128 devices in a mesh: row: 4 (over y_lo, core), col: 32 (over y_hi, x, z).
Axes of the slice: x: 4, y: 4 (y_hi: 2, y_lo: 2; y = y_hi * 2 + y_lo), z: 4, core: 2. Of those that a mesh axis runs over, the one named last changes fastest.
Arguments:
- fringes: bfloat16 [32768, 32768], P(('row', 'col')), may hold values from -24 to 24
- lobe_bounds: int32 [64, 2], replicated, may hold values from 0 to 4096, as said below
- zone_index: int32 [1024, 64], P(('row', 'col')), may hold values from 0 to 4095
- zone_table: float32 [4, 4096], P(None, ('row', 'col')), may hold values from -6 to 6
Outputs:
- heights: bfloat16 [16384, 32768], P(('row', 'col'))
The draws below stay inside these ranges and needn't reach their ends.
Inputs may be any that keep to these rules, and one draw needn't show every extreme that they name: For every band t, lobe_bounds[t, 0] < lobe_bounds[t, 1]; some band starts at 0 and some band ends at 4096.
All inputs are finite; a program needn't handle non-finite values.
Results may differ from the reference program's by a relative error of at most 0.023.
Values may be sent and summed in bfloat16 or wider, within the bound.
A program may use at most 128 MiB of HBM per device.

```python
import math
import jax
import jax.numpy as jnp
from jax import lax

W = 32768
H = 32768
W1 = 128
H1 = 128
KY_TILES = 64
ZB_R = 16
ZB_C = 512
LOBE = 4096
LOBE_START = 4096
NZONES = 4096


def draw_lobe_bounds(key, part):
    lower_key, width_key, zero_key, full_key = jax.random.split(key, 4)
    lower_edge = jax.random.randint(lower_key, (KY_TILES,), 0, LOBE // 2, dtype=jnp.int32)
    widths = jax.random.randint(width_key, (KY_TILES,), LOBE // 4, LOBE // 2 + 1, dtype=jnp.int32)
    upper_edge = lower_edge + widths
    zero_tile = jax.random.randint(zero_key, (), 0, KY_TILES, dtype=jnp.int32)
    full_tile = (zero_tile + 1 + jax.random.randint(full_key, (), 0, KY_TILES - 1, dtype=jnp.int32)) % KY_TILES
    tile_index = jnp.arange(KY_TILES, dtype=jnp.int32)
    lower_edge = jnp.where(tile_index == zero_tile, 0, lower_edge)
    upper_edge = jnp.where(tile_index == full_tile, LOBE, upper_edge)
    return jnp.stack([lower_edge, upper_edge], axis=1).astype(jnp.int32)


def plant(drawn, rng, smallest, high):
    place = [jax.random.randint(jax.random.fold_in(rng, axis), (), 0, length) for axis, length in enumerate(drawn.shape)]
    main_axis = drawn.shape.index(max(drawn.shape))
    neighbour = place[:main_axis] + [(place[main_axis] + 1) % drawn.shape[main_axis]] + place[main_axis + 1:]
    return drawn.at[tuple(place)].set(smallest).at[tuple(neighbour)].set(high)


def level_of(stream_key, extent, cuts, smallest, top_value):
    def one(dim, blocks):
        steps = jax.random.uniform(jax.random.fold_in(jax.random.fold_in(stream_key, 6), dim), (blocks,), jnp.float32, smallest / len(cuts), top_value / len(cuts))
        return jnp.repeat(jnp.exp(steps), extent[dim] // blocks).reshape((-1,) + (1,) * (len(extent) - dim - 1))

    gain = one(*cuts[0])
    for cut in cuts[1:]:
        gain = gain * one(*cut)
    return gain


def centred(key, dims, width, reach, cuts=(), held_as=jnp.bfloat16):
    values = width * jax.random.normal(key, dims, jnp.float32)
    if cuts:
        values = values * level_of(key, dims, cuts, -0.22, 0.18)
    return jnp.clip(values, -reach, reach).astype(held_as)


def setup_inputs(seed: int = 0) -> dict:
    streams_of = jax.random.split(jax.random.key(seed), 5)
    fringes = centred(streams_of[0], (H, W), 4.0, 24.0, ((0, 128),))
    lobe_bounds = draw_lobe_bounds(jax.random.fold_in(streams_of[4], 71), 0)
    zone_index = plant(jax.random.randint(streams_of[2], (H // (2 * ZB_R), W // ZB_C), 0, NZONES), jax.random.fold_in(streams_of[2], 1), 0, NZONES - 1).astype(jnp.int32)
    zone_table = centred(streams_of[3], (4, NZONES), 1.0, 6.0, ((1, 128),), jnp.float32)
    return {"fringes": fringes, "lobe_bounds": lobe_bounds, "zone_index": zone_index, "zone_table": zone_table}


damping_floor = 0.5

def phase_pair(first_count, second_count, period, offset):
    first_index = jnp.arange(first_count, dtype=jnp.int32)[:, None]
    second_index = jnp.arange(second_count, dtype=jnp.int32)[None, :] + offset
    turn_count = first_index * second_index % period
    angles = turn_count.astype(jnp.float32) * (2.0 * math.pi / period)
    return (jnp.cos(angles), jnp.sin(angles))

def table_pair(first_count, second_count, period, offset):
    cosine, sine_part = phase_pair(first_count, second_count, period, offset)
    return (cosine.astype(jnp.bfloat16), sine_part.astype(jnp.bfloat16))

def complex_mix(pattern, real_part, imag_part, cosine, sine_part, direction):
    real_data = real_part.astype(jnp.float32)
    imag_data = imag_part.astype(jnp.float32)
    cos_data = cosine.astype(jnp.float32)
    sin_data = sine_part.astype(jnp.float32)
    real_cos = jnp.einsum(pattern, real_data, cos_data)
    imag_sin = jnp.einsum(pattern, imag_data, sin_data)
    imag_cos = jnp.einsum(pattern, imag_data, cos_data)
    real_sin = jnp.einsum(pattern, real_data, sin_data)
    return (real_cos - direction * imag_sin, imag_cos + direction * real_sin)

def apply_twist(real_part, imag_part, cosine, sine_part, direction):
    out_real = real_part * cosine - direction * (imag_part * sine_part)
    out_imag = imag_part * cosine + direction * (real_part * sine_part)
    return (out_real, out_imag)

def row_forward(rows_block):
    row_total = rows_block.shape[0]
    shaped = rows_block.reshape(row_total, W1, W // W1).astype(jnp.float32)
    cosine, sine_part = table_pair(W1, W1, W1, 0)
    first_real = jnp.einsum('rab,ak->rkb', shaped, cosine.astype(jnp.float32))
    first_imag = -jnp.einsum('rab,ak->rkb', shaped, sine_part.astype(jnp.float32))
    twist_real, twist_imag = phase_pair(W1, W // W1, W, 0)
    middle_real, middle_imag = apply_twist(first_real, first_imag, twist_real, twist_imag, -1.0)
    middle_real = middle_real.astype(jnp.bfloat16)
    middle_imag = middle_imag.astype(jnp.bfloat16)
    cosine, sine_part = table_pair(W // W1, LOBE // W1, W // W1, LOBE_START // W1)
    lobe_real, lobe_imag = complex_mix('rkb,bj->rjk', middle_real, middle_imag, cosine, sine_part, -1.0)
    return jnp.stack([lobe_real, lobe_imag]).reshape(2, row_total, LOBE).astype(jnp.bfloat16)

def column_pass(columns, column_index, lower_edge, upper_edge):
    col_total = columns.shape[1]
    second_len = H // H1
    shaped_real = columns[0].reshape(col_total, H1, second_len)
    shaped_imag = columns[1].reshape(col_total, H1, second_len)
    cosine, sine_part = table_pair(H1, H1, H1, 0)
    first_real, first_imag = complex_mix('cab,ak->ckb', shaped_real, shaped_imag, cosine, sine_part, -1.0)
    twist_real, twist_imag = phase_pair(H1, second_len, H, 0)
    middle_real, middle_imag = apply_twist(first_real, first_imag, twist_real, twist_imag, -1.0)
    middle_real = middle_real.astype(jnp.bfloat16)
    middle_imag = middle_imag.astype(jnp.bfloat16)
    cosine, sine_part = table_pair(second_len, second_len, second_len, 0)
    spectrum_real, spectrum_imag = complex_mix('ckb,bm->cmk', middle_real, middle_imag, cosine, sine_part, -1.0)
    spectrum_real = spectrum_real.reshape(col_total, H)
    spectrum_imag = spectrum_imag.reshape(col_total, H)
    lower_rows = jnp.repeat(lower_edge, H // KY_TILES)
    upper_rows = jnp.repeat(upper_edge, H // KY_TILES)
    keep_mask = (column_index[:, None] >= lower_rows[None, :]) & (column_index[:, None] < upper_rows[None, :])
    masked_real = jnp.where(keep_mask, spectrum_real, 0.0)
    masked_imag = jnp.where(keep_mask, spectrum_imag, 0.0)
    half_rows = H // 2
    fold_scale = 1.0 / (H * W)
    folded_real = ((masked_real[:, :half_rows] + masked_real[:, half_rows:]) * fold_scale).astype(jnp.bfloat16)
    folded_imag = ((masked_imag[:, :half_rows] + masked_imag[:, half_rows:]) * fold_scale).astype(jnp.bfloat16)
    fold_len = second_len // 2
    folded_real = folded_real.reshape(col_total, fold_len, H1)
    folded_imag = folded_imag.reshape(col_total, fold_len, H1)
    cosine, sine_part = table_pair(fold_len, fold_len, fold_len, 0)
    half_real, half_imag = complex_mix('cmk,mq->cqk', folded_real, folded_imag, cosine, sine_part, 1.0)
    twist_real, twist_imag = phase_pair(fold_len, H1, half_rows, 0)
    middle_real, middle_imag = apply_twist(half_real, half_imag, twist_real, twist_imag, 1.0)
    middle_real = middle_real.astype(jnp.bfloat16)
    middle_imag = middle_imag.astype(jnp.bfloat16)
    cosine, sine_part = table_pair(H1, H1, H1, 0)
    out_real, out_imag = complex_mix('cqk,kp->cpq', middle_real, middle_imag, cosine, sine_part, 1.0)
    return jnp.stack([out_real, out_imag]).reshape(2, col_total, half_rows).astype(jnp.bfloat16)

def height_map(field_real, field_imag, coefficients):
    magnitude = jnp.sqrt(field_real * field_real + field_imag * field_imag)
    sine_value = field_imag / jnp.maximum(magnitude, damping_floor)
    row_total = field_real.shape[0]
    sine_value = sine_value.reshape(row_total // ZB_R, ZB_R, W // ZB_C, ZB_C)
    expanded = coefficients[:, :, None, :, None]
    heights = expanded[0] + sine_value * (expanded[1] + sine_value * (expanded[2] + sine_value * expanded[3]))
    return heights.reshape(row_total, W).astype(jnp.bfloat16)

def row_inverse(field_rows, coefficients):
    row_total = field_rows.shape[1]
    shaped_real = field_rows[0].reshape(row_total, LOBE // W1, W1)
    shaped_imag = field_rows[1].reshape(row_total, LOBE // W1, W1)
    cosine, sine_part = table_pair(LOBE // W1, W // W1, W // W1, 0)
    pixel_real, pixel_imag = complex_mix('rjk,jq->rkq', shaped_real, shaped_imag, cosine, sine_part, 1.0)
    twist_real, twist_imag = phase_pair(W1, W // W1, W, 0)
    middle_real, middle_imag = apply_twist(pixel_real, pixel_imag, twist_real, twist_imag, 1.0)
    middle_real = middle_real.astype(jnp.bfloat16)
    middle_imag = middle_imag.astype(jnp.bfloat16)
    cosine, sine_part = table_pair(W1, W1, W1, 0)
    field_real, field_imag = complex_mix('rkq,kp->rpq', middle_real, middle_imag, cosine, sine_part, 1.0)
    return height_map(field_real.reshape(row_total, W), field_imag.reshape(row_total, W), coefficients)

def reference(fringes, lobe_bounds, zone_index, zone_table):
    row_block = min(256, H)
    lobe_blocks = lax.map(row_forward, fringes.reshape(H // row_block, row_block, W))
    lobe_cols = lobe_blocks.transpose(1, 3, 0, 2).reshape(2, LOBE, H)
    col_block = min(128, LOBE)
    col_groups = lobe_cols.reshape(2, LOBE // col_block, col_block, H).transpose(1, 0, 2, 3)
    index_groups = jnp.arange(LOBE, dtype=jnp.int32).reshape(LOBE // col_block, col_block)

    def column_group(pieces):
        return column_pass(pieces[0], pieces[1], lobe_bounds[:, 0], lobe_bounds[:, 1])
    field_groups = lax.map(column_group, (col_groups, index_groups))
    half_rows = H // 2
    field_rows = field_groups.transpose(1, 3, 0, 2).reshape(2, half_rows, LOBE)
    out_block = math.gcd(half_rows, 128 * ZB_R)
    row_groups = field_rows.reshape(2, half_rows // out_block, out_block, LOBE).transpose(1, 0, 2, 3)
    zone_groups = zone_index.reshape(half_rows // out_block, out_block // ZB_R, W // ZB_C)

    def height_group(pieces):
        coefficients = zone_table[:, pieces[1]]
        return row_inverse(pieces[0], coefficients)
    heights = lax.map(height_group, (row_groups, zone_groups))
    return heights.reshape(half_rows, W)
```

```python
import functools
import math

import jax
import jax.numpy as jnp
import ml_dtypes
import numpy as np
from jax import lax
from jax.experimental import pallas as pl
from jax.experimental.pallas import tpu as pltpu
from jax.sharding import PartitionSpec as P

W = 32768
H = 32768
LOBE = 4096
LOBE_START = 4096
DEVICES = 128
ROWS = H // DEVICES
HALF = ROWS // 2
KEPT = H // (2 * DEVICES)
GROUP = 32
ZB_R = 16

damping_floor = 0.5
bf16 = jnp.bfloat16
f32 = jnp.float32
MESH = pl.DeviceIdType.MESH


def turns(first, second, period):
    angles = (np.outer(first, second) % period).astype(np.float64) * (2.0 * math.pi / period)
    return np.cos(angles), np.sin(angles)


def make_tables():
    n4, n8, n16, n32 = (np.arange(n) for n in (4, 8, 16, 32))
    n128, n256, n1024, n2048 = (np.arange(n) for n in (128, 256, 1024, 2048))
    half = {}
    full = {}
    cosine, sine = turns(n16, n16, 16)
    half["row_a"] = np.kron(np.concatenate([cosine[:9], -sine[1:8]], 0), np.eye(16))
    cosine, sine = turns(n16, n2048, W)
    full["row_twist"] = np.broadcast_to(
        np.stack([cosine, sine], 1)[:, :, None, :], (16, 2, 8, 2048)
    )
    sides = []
    for odd in range(2):
        cosine, sine = turns(n1024, LOBE_START // 16 + 2 * n128 + odd, 2048)
        real = np.concatenate([cosine, sine], 0).reshape(2048, 4, 2, 16)
        imag = np.concatenate([-sine, cosine], 0).reshape(2048, 4, 2, 16)
        sides.append(np.stack([real, imag], 3).reshape(2048, 256))
    half["row_b"] = np.stack(sides)
    cosine, sine = turns(n128, n128, 128)
    half["col_a"] = np.block([[cosine, sine], [-sine, cosine]])
    half["col_m"] = np.block([[cosine, sine], [-sine, cosine]])
    half["col_p"] = np.block([[cosine, -sine], [sine, cosine]])
    cosine, sine = turns(n128, n256, H)
    full["col_twist"] = np.stack([cosine, sine])
    cosine, sine = turns(n256, n256, 256)
    half["col_b"] = np.block([[cosine, -sine], [sine, cosine]])
    cosine, sine = turns(n128, n128, H // 2)
    full["half_twist"] = np.stack([cosine, sine])
    cosine, sine = turns(n128, n1024, 1024)
    real = np.stack([cosine.reshape(128, 8, 128), sine.reshape(128, 8, 128)], 2).reshape(128, 2048)
    imag = np.stack([-sine.reshape(128, 8, 128), cosine.reshape(128, 8, 128)], 2).reshape(128, 2048)
    half["pix_j"] = np.stack([real.reshape(4, 2, 16, 2048), imag.reshape(4, 2, 16, 2048)], 2).reshape(
        256, 2048
    )
    cosine, sine = turns(n32, n1024, W)
    full["pix_twist"] = np.broadcast_to(
        np.stack([cosine, sine], 1)[:, :, None, :], (32, 2, 8, 1024)
    )
    mats = []
    for p0 in range(4):
        cosine, sine = turns(p0 + 4 * n8, n8, 32)
        block = np.stack(
            [np.stack([cosine, -sine], -1), np.stack([sine, cosine], -1)], 1
        ).reshape(16, 16)
        mats.append(np.kron(block, np.eye(16)))
    half["pix_k"] = np.stack(mats)
    made = {name: value.astype(ml_dtypes.bfloat16) for name, value in half.items()}
    made.update({name: np.ascontiguousarray(value, np.float32) for name, value in full.items()})
    return made


def dot(left, right):
    return jnp.dot(left, right, preferred_element_type=f32)


def at(start, size):
    return pl.ds(pl.multiple_of(start, size), size)


def row_first(block, tile, rows16, mat, twist, mid):
    sides = []
    for upper in range(2):
        sides.append(
            jnp.concatenate(
                [
                    block[pl.ds(rows16 * 16, 16), at(2048 * a + 1024 * upper + tile * 128, 128)]
                    for a in range(16)
                ],
                axis=0,
            )
        )
    mixed = dot(mat[...], jnp.concatenate(sides, axis=1))
    low = at(tile * 128, 128)
    high = at(1024 + tile * 128, 128)

    def part(index, upper):
        return mixed[index * 16 : (index + 1) * 16, upper * 128 : (upper + 1) * 128]

    def factor(k, index, place):
        value = twist[k, index, :, place]
        return jnp.concatenate([value, value], axis=0)

    for k in range(16):
        twisted = []
        for upper, place in ((0, low), (1, high)):
            source = k if k <= 8 else 16 - k
            real = part(source, upper)
            if k == 0:
                twisted.append((real, None))
                continue
            cosine = factor(k, 0, place)
            sine = factor(k, 1, place)
            if k == 8:
                twisted.append((real * cosine, -(real * sine)))
                continue
            imag = part(source + 8, upper)
            if k < 8:
                twisted.append((real * cosine + imag * sine, imag * cosine - real * sine))
            else:
                twisted.append((real * cosine - imag * sine, -(imag * cosine + real * sine)))
        (real0, imag0), (real1, imag1) = twisted
        rows = pl.ds(k * GROUP + rows16 * 16, 16)
        mid[0, rows, low] = (real0 + real1).astype(bf16)
        mid[1, rows, low] = (real0 - real1).astype(bf16)
        if imag0 is None:
            mid[0, rows, high] = jnp.zeros((16, 128), bf16)
            mid[1, rows, high] = jnp.zeros((16, 128), bf16)
        else:
            mid[0, rows, high] = (imag0 + imag1).astype(bf16)
            mid[1, rows, high] = (imag0 - imag1).astype(bf16)


def row_second(mid, odd, block, mat, lobe, group):
    rows = 8 * GROUP
    mixed = dot(mid[odd, at(block * rows, rows), :], mat[odd]).astype(bf16)
    for k in range(8):
        lobe[odd * 16 + block * 8 + k, at(group * GROUP, GROUP), :] = mixed[
            k * GROUP : (k + 1) * GROUP
        ]


def column_pair(pair, chunk, first_column, gather, mats, twists, edges, field):
    col_a, col_b, col_m, col_p = mats
    col_twist, half_twist = twists
    middles = []
    for u in range(2):
        j = pair * 2 + u
        parts = []
        for part in range(2):
            parts.append(
                jnp.concatenate(
                    [gather[h, pl.ds(part * 16 + j, DEVICES, stride=32), :] for h in range(2)],
                    axis=1,
                )
            )
        mixed = dot(col_a[...], jnp.concatenate(parts, axis=0).astype(bf16))
        real, imag = mixed[:128], mixed[128:]
        cosine, sine = col_twist[0], col_twist[1]
        middles.append(
            jnp.concatenate(
                [
                    (real * cosine + imag * sine).astype(bf16),
                    (imag * cosine - real * sine).astype(bf16),
                ],
                axis=1,
            )
        )
    spectrum = dot(jnp.concatenate(middles, axis=0), col_b[...])
    folded = []
    for u in range(2):
        column = first_column + 32 * (chunk * 16 + pair * 2 + u)
        keep = jnp.where((column >= edges[0:1, :]) & (column < edges[1:2, :]), 1.0 / (H * W), 0.0)
        rows = spectrum[u * 128 : (u + 1) * 128]
        folded.append(
            jnp.concatenate(
                [
                    (
                        rows[:, part * 256 : part * 256 + 128] * keep[:, :128]
                        + rows[:, part * 256 + 128 : part * 256 + 256] * keep[:, 128:]
                    ).astype(bf16)
                    for part in range(2)
                ],
                axis=1,
            )
        )
    halves = dot(jnp.concatenate(folded, axis=0), col_m[...])
    cosine, sine = half_twist[0], half_twist[1]
    terms = []
    for u in range(2):
        rows = halves[u * 128 : (u + 1) * 128]
        real, imag = rows[:, :128], rows[:, 128:]
        terms.append(
            jnp.concatenate(
                [
                    (real * cosine - imag * sine).astype(bf16),
                    (imag * cosine + real * sine).astype(bf16),
                ],
                axis=0,
            )
        )
    out = dot(col_p[...], jnp.concatenate(terms, axis=1))
    for u in range(2):
        field[at((pair * 2 + u) * 256, 256), :] = out[:, u * 128 : (u + 1) * 128]


def spectrum_kernel(
    fringes, edges, zones, row_a, row_twist, row_b, col_a, col_b, col_m, col_p, col_twist, half_twist,
    out, zones_out,
    block, mid, lobe, send_a, send_b, recv_a, recv_b, gather, field, send_c,
    load_sem, send_sem, recv_sem, own_sem,
):
    my_row = lax.axis_index("row")
    my_col = lax.axis_index("col")
    cols = lax.axis_size("col")
    me = my_row * cols + my_col

    def place(device):
        return (device // cols, lax.rem(device, cols))

    barrier = pltpu.get_barrier_semaphore()

    def greet(i, carry):
        pl.semaphore_signal(
            barrier, inc=1, device_id=place(lax.rem(me + i, DEVICES)), device_id_type=MESH
        )
        return carry

    def load(group, slot):
        return pltpu.make_async_copy(
            fringes.at[at(group * GROUP, GROUP), :], block.at[slot], load_sem.at[slot]
        )

    def send(source, target, device, index):
        @pl.when(device != me)
        def _():
            pltpu.make_async_remote_copy(
                src_ref=source, dst_ref=target, send_sem=send_sem.at[index],
                recv_sem=recv_sem.at[index], device_id=place(device), device_id_type=MESH,
            ).start()

        @pl.when(device == me)
        def _():
            pltpu.make_async_copy(source, target, own_sem.at[index]).start()


    def wait_recv(buffer, index):
        others = buffer.at[pl.ds(0, DEVICES - 1)]
        pltpu.make_async_copy(others, others, recv_sem.at[index]).wait()
        pltpu.make_async_copy(buffer.at[0], buffer.at[0], own_sem.at[index]).wait()

    def wait_send(buffer, index):
        others = buffer.at[pl.ds(0, DEVICES - 1)]
        pltpu.make_async_copy(others, others, send_sem.at[index]).wait()

    load(0, 0).start()
    lax.fori_loop(1, DEVICES, greet, 0)

    groups = HALF // GROUP
    for h in range(2):

        def group_step(g, carry, h=h):
            index = h * groups + g
            slot = lax.rem(index, 2)

            @pl.when(index < 2 * groups - 1)
            def _():
                load(index + 1, 1 - slot).start()

            load(index, slot).wait()

            def piece(i, inner):
                row_second(
                    mid.at[1 - slot], i // 2, lax.rem(i, 2), row_b, lobe, jnp.maximum(g - 1, 0)
                )
                for v in range(2):
                    for rows16 in range(2):
                        row_first(
                            block.at[slot], i * 2 + v, rows16, row_a, row_twist, mid.at[slot]
                        )
                return inner

            lax.fori_loop(0, 4, piece, 0)
            return carry

        lax.fori_loop(0, groups, group_step, 0)

        def last_piece(i, carry):
            row_second(mid.at[1], i // 2, lax.rem(i, 2), row_b, lobe, groups - 1)
            return carry

        lax.fori_loop(0, 4, last_piece, 0)

        if h == 0:
            pl.semaphore_wait(barrier, DEVICES - 1)

            def send_first(i, carry):
                k = lax.rem(me // 4 + i, 32)
                flipped = lobe[k].T
                for j in range(4):
                    send_a[k * 4 + j] = flipped[j * 64 : (j + 1) * 64]
                for j in range(4):
                    device = k * 4 + lax.rem(me + j, 4)
                    send(send_a.at[device], recv_a.at[me], device, 0)
                return carry

            lax.fori_loop(0, 32, send_first, 0)

            def send_zones(i, carry):
                device = lax.rem(me + i, DEVICES)
                send(zones.at[0], zones_out.at[me], device, 4)
                return carry

            lax.fori_loop(0, DEVICES, send_zones, 0)
        else:

            def send_second(i, carry):
                k = lax.rem(me // 4 + i, 32)
                flipped = lobe[k].T
                for j in range(4):
                    for chunk in range(2):
                        send_b[chunk, k * 4 + j] = flipped[
                            j * 64 + chunk * 32 : j * 64 + chunk * 32 + 32
                        ]
                for j in range(4):
                    device = k * 4 + lax.rem(me + j, 4)
                    send(send_b.at[0, device], recv_b.at[0, me], device, 1)
                return carry

            lax.fori_loop(0, 32, send_second, 0)

            def send_third(i, carry):
                device = lax.rem(me + i, DEVICES)
                send(send_b.at[1, device], recv_b.at[1, me], device, 2)
                return carry

            lax.fori_loop(0, DEVICES, send_third, 0)

    first_column = me // 4 + 32 * 32 * lax.rem(me, 4)
    wait_recv(recv_a, 0)
    for chunk in range(2):
        wait_recv(recv_b.at[chunk], 1 + chunk)

        def spread(i, carry, chunk=chunk):
            for u in range(8):
                a = i * 8 + u
                gather[0, at(a * 32, 32), :] = recv_a[a, chunk * 32 : chunk * 32 + 32, :].astype(f32)
                gather[1, at(a * 32, 32), :] = recv_b[chunk, a].astype(f32)
            return carry

        lax.fori_loop(0, DEVICES // 8, spread, 0)

        def pair_step(pair, carry, chunk=chunk):
            column_pair(
                pair, chunk, first_column, gather, (col_a, col_b, col_m, col_p),
                (col_twist, half_twist), edges, field,
            )
            return carry

        lax.fori_loop(0, 8, pair_step, 0)

        def send_field(i, carry, chunk=chunk):
            device = lax.rem(me + i, DEVICES)
            for part in range(2):
                send_c[chunk, device, part * 16 : part * 16 + 16, :] = field[
                    pl.ds(part * 128 + device, 16, stride=256), :
                ].astype(bf16)
            send(send_c.at[chunk, device], out.at[chunk, me], device, 5 + chunk)
            return carry

        lax.fori_loop(0, DEVICES, send_field, 0)

    wait_send(send_a, 0)
    wait_send(send_b.at[0], 1)
    wait_send(send_b.at[1], 2)
    wait_send(send_c.at[0], 5)
    wait_send(send_c.at[1], 6)
    wait_recv(out.at[0], 5)
    wait_recv(out.at[1], 6)
    wait_send(zones_out, 4)
    wait_recv(zones_out, 4)


def exchange(fringes, edges, zones, tables):
    names = ("row_a", "row_twist", "row_b", "col_a", "col_b", "col_m", "col_p", "col_twist", "half_twist")
    return pl.pallas_call(
        spectrum_kernel,
        out_shape=(
            jax.ShapeDtypeStruct((2, DEVICES, 32, KEPT), bf16),
            jax.ShapeDtypeStruct((DEVICES, 1, 128), f32),
        ),
        in_specs=[pl.BlockSpec(memory_space=pl.ANY)]
        + [pl.BlockSpec(memory_space=pltpu.VMEM)] * (2 + len(names)),
        out_specs=(pl.BlockSpec(memory_space=pl.ANY),) * 2,
        scratch_shapes=[
            pltpu.VMEM((2, GROUP, W), bf16),
            pltpu.VMEM((2, 2, 16 * GROUP, 2048), bf16),
            pltpu.VMEM((32, HALF, 256), bf16),
            pltpu.VMEM((DEVICES, 64, HALF), bf16),
            pltpu.VMEM((2, DEVICES, 32, HALF), bf16),
            pltpu.VMEM((DEVICES, 64, HALF), bf16),
            pltpu.VMEM((2, DEVICES, 32, HALF), bf16),
            pltpu.VMEM((2, DEVICES * 32, 128), f32),
            pltpu.VMEM((16 * 256, 128), f32),
            pltpu.VMEM((2, DEVICES, 32, KEPT), bf16),
            pltpu.SemaphoreType.DMA((2,)),
            pltpu.SemaphoreType.DMA((7,)),
            pltpu.SemaphoreType.DMA((7,)),
            pltpu.SemaphoreType.DMA((7,)),
        ],
        compiler_params=pltpu.CompilerParams(
            collective_id=0, has_side_effects=True, vmem_limit_bytes=60 << 20
        ),
        name="spectrum",
    )(fringes, edges, zones, *[tables[name] for name in names])


def height_kernel(zone_index, zone_table, received, pix_j, pix_twist, pix_k, out, rows, terms):
    group = pl.program_id(0)

    @pl.when(group == 0)
    def _():
        def flip(k, carry):
            stacked = jnp.concatenate(
                [received[chunk, k * 4 + j] for j in range(4) for chunk in range(2)], axis=0
            )
            rows[k] = stacked.T
            return carry

        lax.fori_loop(0, 32, flip, 0)

    left = rows[:, at(group * 16, 16), :].reshape(512, 256)

    def quarter(q, carry):
        for u in range(2):
            tile = q * 2 + u
            lanes = at(tile * 128, 128)
            mixed = dot(left, pix_j[:, at(tile * 256, 256)])
            for k0 in range(8):
                real = []
                imag = []
                for k1 in range(4):
                    k = k1 * 8 + k0
                    re = mixed[k * 16 : (k + 1) * 16, :128]
                    im = mixed[k * 16 : (k + 1) * 16, 128:]
                    if k:
                        cosine = pix_twist[k, 0, :, lanes]
                        sine = pix_twist[k, 1, :, lanes]
                        cosine = jnp.concatenate([cosine, cosine], axis=0)
                        sine = jnp.concatenate([sine, sine], axis=0)
                        re, im = re * cosine - im * sine, im * cosine + re * sine
                    real.append(re)
                    imag.append(im)
                even_re, even_im = real[0] + real[2], imag[0] + imag[2]
                odd_re, odd_im = real[1] + real[3], imag[1] + imag[3]
                gap_re, gap_im = real[0] - real[2], imag[0] - imag[2]
                side_re, side_im = real[1] - real[3], imag[1] - imag[3]
                results = (
                    (even_re + odd_re, even_im + odd_im),
                    (gap_re - side_im, gap_im + side_re),
                    (even_re - odd_re, even_im - odd_im),
                    (gap_re + side_im, gap_im - side_re),
                )
                for p0 in range(4):
                    for part in range(2):
                        terms[p0, pl.ds(k0 * 32 + part * 16, 16), u * 128 : u * 128 + 128] = results[
                            p0
                        ][part].astype(bf16)
        for p0 in range(4):
            mixed = dot(pix_k[p0], terms[p0])
            for p1 in range(8):
                p = p0 + 4 * p1
                real = mixed[p1 * 32 : p1 * 32 + 16]
                imag = mixed[p1 * 32 + 16 : p1 * 32 + 32]
                sine = imag * jnp.minimum(
                    lax.rsqrt(real * real + imag * imag), 1.0 / damping_floor
                )
                zone = zone_index[group, 2 * p + q // 2]
                source = zone // 32
                place = lax.rem(zone, 32)
                e0, e1, e2, e3 = (zone_table[source, place + 32 * r] for r in range(4))
                heights = e0 + sine * (e1 + sine * (e2 + sine * e3))
                out[:, at(1024 * p + q * 256, 256)] = heights.astype(bf16)
        return carry

    lax.fori_loop(0, 4, quarter, 0)


def height_map(zone_index, zone_table, received, tables):
    return pl.pallas_call(
        height_kernel,
        grid=(KEPT // ZB_R,),
        out_shape=jax.ShapeDtypeStruct((KEPT, W), bf16),
        in_specs=[pl.BlockSpec(memory_space=pltpu.SMEM)] * 2
        + [pl.BlockSpec(memory_space=pltpu.VMEM)] * 4,
        out_specs=pl.BlockSpec((ZB_R, W), lambda g: (g, 0)),
        scratch_shapes=[pltpu.VMEM((32, KEPT, 256), bf16), pltpu.VMEM((4, 256, 256), bf16)],
        compiler_params=pltpu.CompilerParams(vmem_limit_bytes=48 << 20),
        name="heights",
    )(zone_index, zone_table, received, tables["pix_j"], tables["pix_twist"], tables["pix_k"])


def body(tables, fringes, lobe_bounds, zone_index, zone_table):
    edges = jnp.repeat(lobe_bounds.T, 4, axis=1)
    zones = zone_table.reshape(1, 1, 128)
    received, zones = exchange(fringes, edges, zones, tables)
    return height_map(zone_index, zones.reshape(DEVICES, 128), received, tables)


def solution(mesh):
    placed = (P(("row", "col"), None), P(), P(("row", "col"), None), P(None, ("row", "col")))
    return jax.shard_map(
        functools.partial(body, make_tables()),
        mesh=mesh,
        in_specs=placed,
        out_specs=P(("row", "col"), None),
        check_vma=False,
    )
```

```python
import functools
import math

import jax
import jax.numpy as jnp
import ml_dtypes
import numpy as np
from jax import lax
from jax.experimental import pallas as pl
from jax.experimental.pallas import tpu as pltpu
from jax.sharding import PartitionSpec as P

W = 32768
H = 32768
LOBE = 4096
LOBE_START = 4096
DEVICES = 128
ROWS = H // DEVICES
HALF = ROWS // 2
KEPT = H // (2 * DEVICES)
GROUP = 32
ZB_R = 16

damping_floor = 0.5
bf16 = jnp.bfloat16
f32 = jnp.float32
MESH = pl.DeviceIdType.MESH


def turns(first, second, period):
    angles = (np.outer(first, second) % period).astype(np.float64) * (2.0 * math.pi / period)
    return np.cos(angles), np.sin(angles)


def lane_tiles(matrix):
    shape = matrix.shape
    return np.moveaxis(matrix.reshape(*shape[:-1], shape[-1] // 128, 128), -2, -3)


def by_tile(rows):
    first, two, length = rows.shape
    return np.broadcast_to(
        rows.reshape(first, two, length // 128, 1, 128), (first, two, length // 128, 8, 128)
    )


def make_tables():
    n4, n8, n16, n32 = (np.arange(n) for n in (4, 8, 16, 32))
    n128, n256, n1024, n2048 = (np.arange(n) for n in (128, 256, 1024, 2048))
    half = {}
    full = {}
    cosine, sine = turns(n16, n16, 16)
    half["row_a"] = np.kron(np.concatenate([cosine[:9], -sine[1:8]], 0), np.eye(16))
    cosine, sine = turns(n16, n2048, W)
    full["row_twist"] = by_tile(np.stack([cosine, sine], 1))
    sides = []
    for odd in range(2):
        cosine, sine = turns(n1024, LOBE_START // 16 + 2 * n128 + odd, 2048)
        real = np.concatenate([cosine, sine], 0).reshape(2048, 4, 2, 16)
        imag = np.concatenate([-sine, cosine], 0).reshape(2048, 4, 2, 16)
        sides.append(np.stack([real, imag], 3).transpose(0, 2, 1, 3, 4).reshape(2048, 256))
    half["row_b"] = np.stack(sides)
    cosine, sine = turns(n128, n128, 128)
    half["col_a"] = np.block([[cosine, sine], [-sine, cosine]])
    half["col_m"] = np.block([[cosine, sine], [-sine, cosine]])
    half["col_p"] = np.block([[cosine, -sine], [sine, cosine]])
    cosine, sine = turns(n128, n256, H)
    full["col_twist"] = np.stack([cosine, sine])
    cosine, sine = turns(n256, n256, 256)
    half["col_b"] = np.block([[cosine, -sine], [sine, cosine]])
    cosine, sine = turns(n128, n128, H // 2)
    full["half_twist"] = np.stack([cosine, sine])
    cosine, sine = turns(n128, n1024, 1024)
    real = np.stack([cosine.reshape(128, 8, 128), sine.reshape(128, 8, 128)], 2).reshape(128, 2048)
    imag = np.stack([-sine.reshape(128, 8, 128), cosine.reshape(128, 8, 128)], 2).reshape(128, 2048)
    half["pix_j"] = np.stack([real.reshape(4, 2, 16, 2048), imag.reshape(4, 2, 16, 2048)], 2).reshape(
        256, 2048
    )
    cosine, sine = turns(n32, n1024, W)
    full["pix_twist"] = by_tile(np.stack([cosine, sine], 1))
    mats = []
    for p0 in range(4):
        cosine, sine = turns(p0 + 4 * n8, n8, 32)
        block = np.stack(
            [np.stack([cosine, -sine], -1), np.stack([sine, cosine], -1)], 1
        ).reshape(16, 16)
        mats.append(np.kron(block, np.eye(16)))
    half["pix_k"] = np.stack(mats)
    made = {name: lane_tiles(value).astype(ml_dtypes.bfloat16) for name, value in half.items()}
    made.update({name: np.ascontiguousarray(value, np.float32) for name, value in full.items()})
    return made


def dot(left, right):
    return jnp.dot(left, right, preferred_element_type=f32)


def joined(tiles):
    return jnp.concatenate([tiles[i] for i in range(tiles.shape[0])], axis=1)


def at(start, size):
    return pl.ds(pl.multiple_of(start, size), size)


def row_first(block, pair, rows16, mat, twist, mid):
    sides = [
        [
            block[pl.ds(rows16 * 16, 16), at(2048 * a + 1024 * upper + pair * 256, 256)]
            for a in range(16)
        ]
        for upper in range(2)
    ]
    left = joined(mat)
    rows = [pl.ds(k * GROUP + rows16 * 16, 16) for k in range(16)]
    for v in range(2):
        tile = pair * 2 + v
        right = jnp.concatenate(
            [
                jnp.concatenate([piece[:, v * 128 : v * 128 + 128] for piece in side], axis=0)
                for side in sides
            ],
            axis=1,
        )
        mixed = dot(left, right)

        def part(index, upper):
            return mixed[index * 16 : (index + 1) * 16, upper * 128 : (upper + 1) * 128]

        def factor(k, index, upper):
            value = twist[k, index, upper * 8 + tile]
            return jnp.concatenate([value, value], axis=0)

        for k in range(16):
            twisted = []
            for upper in range(2):
                source = k if k <= 8 else 16 - k
                real = part(source, upper)
                if k == 0:
                    twisted.append((real, None))
                    continue
                cosine = factor(k, 0, upper)
                sine = factor(k, 1, upper)
                if k == 8:
                    twisted.append((real * cosine, -(real * sine)))
                    continue
                imag = part(source + 8, upper)
                if k < 8:
                    twisted.append((real * cosine + imag * sine, imag * cosine - real * sine))
                else:
                    twisted.append((real * cosine - imag * sine, -(imag * cosine + real * sine)))
            (real0, imag0), (real1, imag1) = twisted
            mid[0, tile, rows[k], :] = (real0 + real1).astype(bf16)
            mid[1, tile, rows[k], :] = (real0 - real1).astype(bf16)
            if imag0 is None:
                mid[0, 8 + tile, rows[k], :] = jnp.zeros((16, 128), bf16)
                mid[1, 8 + tile, rows[k], :] = jnp.zeros((16, 128), bf16)
            else:
                mid[0, 8 + tile, rows[k], :] = (imag0 + imag1).astype(bf16)
                mid[1, 8 + tile, rows[k], :] = (imag0 - imag1).astype(bf16)


def row_second(mid, odd, block, mat, lobe, group):
    rows = 8 * GROUP
    left = jnp.concatenate([mid[odd, t, at(block * rows, rows), :] for t in range(16)], axis=1)
    mixed = dot(left, joined(mat.at[odd])).astype(bf16)
    for k in range(8):
        for chunk in range(2):
            lobe[odd * 16 + block * 8 + k, chunk, at(group * GROUP, GROUP), :] = mixed[
                k * GROUP : (k + 1) * GROUP, chunk * 128 : chunk * 128 + 128
            ]


def column_pair(pair, chunk, first_column, gather, mats, twists, edges, field):
    col_a, col_b, col_m, col_p = mats
    col_twist, half_twist = twists
    middles = []
    for u in range(2):
        j = pair * 2 + u
        parts = []
        for part in range(2):
            parts.append(
                jnp.concatenate(
                    [gather[h, pl.ds(part * 16 + j, DEVICES, stride=32), :] for h in range(2)],
                    axis=1,
                )
            )
        mixed = dot(joined(col_a), jnp.concatenate(parts, axis=0).astype(bf16))
        real, imag = mixed[:128], mixed[128:]
        cosine, sine = col_twist[0], col_twist[1]
        middles.append(
            jnp.concatenate(
                [
                    (real * cosine + imag * sine).astype(bf16),
                    (imag * cosine - real * sine).astype(bf16),
                ],
                axis=1,
            )
        )
    spectrum = dot(jnp.concatenate(middles, axis=0), joined(col_b))
    folded = []
    for u in range(2):
        column = first_column + 32 * (chunk * 16 + pair * 2 + u)
        keep = jnp.where((column >= edges[0]) & (column < edges[1]), 1.0 / (H * W), 0.0)
        rows = spectrum[u * 128 : (u + 1) * 128]
        folded.append(
            jnp.concatenate(
                [
                    (
                        rows[:, part * 256 : part * 256 + 128] * keep[:, :128]
                        + rows[:, part * 256 + 128 : part * 256 + 256] * keep[:, 128:]
                    ).astype(bf16)
                    for part in range(2)
                ],
                axis=1,
            )
        )
    halves = dot(jnp.concatenate(folded, axis=0), joined(col_m))
    cosine, sine = half_twist[0], half_twist[1]
    terms = []
    for u in range(2):
        rows = halves[u * 128 : (u + 1) * 128]
        real, imag = rows[:, :128], rows[:, 128:]
        terms.append(
            jnp.concatenate(
                [
                    (real * cosine - imag * sine).astype(bf16),
                    (imag * cosine + real * sine).astype(bf16),
                ],
                axis=0,
            )
        )
    out = dot(joined(col_p), jnp.concatenate(terms, axis=1))
    for u in range(2):
        field[at((pair * 2 + u) * 256, 256), :] = out[:, u * 128 : (u + 1) * 128]


def spectrum_kernel(
    bounds, fringes, zones, *refs,
):
    given, refs = refs[:9], refs[9:]
    out, zones_out, *refs = refs
    tables, refs = refs[:9], refs[9:]
    row_a, row_twist, row_b, col_a, col_b, col_m, col_p, col_twist, half_twist = tables
    block, mid, lobe, send_a, recv_a, gather, field, send_c, edges, zone_rows, zone_row = refs[:11]
    load_sem, send_sem, recv_sem, own_sem, table_sem = refs[11:]
    table_copies = [
        pltpu.make_async_copy(given[i], tables[i], table_sem.at[i]) for i in range(9)
    ]
    my_row = lax.axis_index("row")
    my_col = lax.axis_index("col")
    cols = lax.axis_size("col")
    me = my_row * cols + my_col

    def place(device):
        return (lax.div(device, cols), lax.rem(device, cols))

    def other(i):
        return lax.rem(me + i, DEVICES)

    barrier = pltpu.get_barrier_semaphore()

    def greet(i, carry):
        pl.semaphore_signal(barrier, inc=1, device_id=place(other(i)), device_id_type=MESH)
        return carry

    def load(group, slot):
        return pltpu.make_async_copy(
            fringes.at[at(group * GROUP, GROUP), :], block.at[slot], load_sem.at[slot]
        )

    def send(source, target, device, index):
        pltpu.make_async_remote_copy(
            src_ref=source, dst_ref=target, send_sem=send_sem.at[index],
            recv_sem=recv_sem.at[index], device_id=place(device), device_id_type=MESH,
        ).start()

    def keep(source, target, index):
        pltpu.make_async_copy(source, target, own_sem.at[index]).start()

    def wait_recv(buffer, index):
        others = buffer.at[pl.ds(0, DEVICES - 1)]
        pltpu.make_async_copy(others, others, recv_sem.at[index]).wait()
        pltpu.make_async_copy(buffer.at[0], buffer.at[0], own_sem.at[index]).wait()

    def wait_send(buffer, index):
        others = buffer.at[pl.ds(0, DEVICES - 1)]
        pltpu.make_async_copy(others, others, send_sem.at[index]).wait()

    load(0, 0).start()
    for copy in table_copies:
        copy.start()
    lax.fori_loop(1, DEVICES, greet, 0)

    lanes = lax.broadcasted_iota(jnp.int32, (1, 256), 1)

    def edge_step(t, carry):
        mine = (lanes >= 4 * t) & (lanes < 4 * t + 4)
        return tuple(jnp.where(mine, bounds[side, t], carry[side]) for side in range(2))

    both = lax.fori_loop(0, 64, edge_step, (jnp.zeros((1, 256), jnp.int32),) * 2)
    edges[0] = both[0]
    edges[1] = both[1]
    zone_rows[...] = jnp.zeros((8, 128), f32)
    zone_rows[0:4, 0:32] = zones[...]
    spread_rows = zone_rows[...]
    zone_row[...] = spread_rows[0:1] + sum(
        pltpu.roll(spread_rows, 32 * r, 1)[r : r + 1] for r in range(1, 4)
    )

    table_copies[0].wait()
    table_copies[1].wait()

    def first_only(group):
        slot = lax.rem(group, 2)
        load(group + 1, 1 - slot).start()
        load(group, slot).wait()

        def piece(pair, carry):
            for rows16 in range(2):
                row_first(block.at[slot], pair, rows16, row_a, row_twist, mid.at[slot])
            return carry

        lax.fori_loop(0, 4, piece, 0)

    def both_steps(group, last):
        slot = lax.rem(group, 2)
        if not last:
            load(group + 1, 1 - slot).start()
        load(group, slot).wait()

        def piece(i, carry):
            row_second(
                mid.at[1 - slot], lax.div(i, 2), lax.rem(i, 2), row_b, lobe, lax.rem(group - 1, 4)
            )
            for rows16 in range(2):
                row_first(block.at[slot], i, rows16, row_a, row_twist, mid.at[slot])
            return carry

        lax.fori_loop(0, 4, piece, 0)

    def second_only(group):
        slot = lax.rem(group, 2)

        def piece(i, carry):
            row_second(mid.at[slot], lax.div(i, 2), lax.rem(i, 2), row_b, lobe, lax.rem(group, 4))
            return carry

        lax.fori_loop(0, 4, piece, 0)

    def send_block(buffer, target, k, low, index):
        for j in range(low, 4):
            device = k * 4 + lax.rem(me + j, 4)
            send(buffer.at[device], target.at[me], device, index)

    def quarter_step(c, carry):
        first_only(2 * c)

        @pl.when(c == 0)
        def _():
            table_copies[2].wait()

        both_steps(2 * c + 1, False)
        second_only(2 * c + 1)

        @pl.when(c == 0)
        def _():
            pl.semaphore_wait(barrier, DEVICES - 1)

        def pack(i):
            k = lax.rem(lax.div(me, 4) + i, 32)
            rows = at(c * 64, 64)
            upper = lobe[k, c, rows, :]
            lower = lobe[k, 1 - c, rows, :]
            flipped = jnp.concatenate([upper, lower], axis=0).T
            for j in range(4):
                send_a[c, k * 4 + j] = flipped[j * 32 : (j + 1) * 32]
            return k

        k = pack(0)
        keep(send_a.at[c, me], recv_a.at[c, me], c)
        send_block(send_a.at[c], recv_a.at[c], k, 1, c)

        def pack_step(i, inner):
            send_block(send_a.at[c], recv_a.at[c], pack(i), 0, c)
            return inner

        lax.fori_loop(1, 32, pack_step, 0)
        return carry

    lax.fori_loop(0, 2, quarter_step, 0)

    keep(zone_row, zones_out.at[me], 4)

    def send_zones(i, carry):
        send(zone_row, zones_out.at[me], other(i), 4)
        return carry

    first_only(4)

    def half_step(g, carry):
        both_steps(g, False)
        return carry

    lax.fori_loop(5, 7, half_step, 0)
    both_steps(7, True)
    second_only(7)

    def pack_half(i):
        k = lax.rem(lax.div(me, 4) + i, 32)
        for chunk in range(2):
            flipped = lobe[k, chunk].T
            for j in range(4):
                send_a[2 + chunk, k * 4 + j] = flipped[j * 32 : (j + 1) * 32]
        return k

    k = pack_half(0)
    keep(send_a.at[2, me], recv_a.at[2, me], 2)
    send_block(send_a.at[2], recv_a.at[2], k, 1, 2)

    def pack_half_step(i, carry):
        send_block(send_a.at[2], recv_a.at[2], pack_half(i), 0, 2)
        return carry

    lax.fori_loop(1, 32, pack_half_step, 0)
    keep(send_a.at[3, me], recv_a.at[3, me], 3)

    def send_last(i, carry):
        send(send_a.at[3, other(i)], recv_a.at[3, me], other(i), 3)
        return carry

    lax.fori_loop(1, DEVICES, send_last, 0)
    lax.fori_loop(1, DEVICES, send_zones, 0)

    first_column = lax.div(me, 4) + 32 * 32 * lax.rem(me, 4)
    low_lanes = lax.broadcasted_iota(jnp.int32, (32, 128), 1) < 64
    for copy in table_copies[3:]:
        copy.wait()
    wait_recv(recv_a.at[0], 0)
    wait_recv(recv_a.at[1], 1)
    for chunk in range(2):
        wait_recv(recv_a.at[2 + chunk], 2 + chunk)

        def spread(i, carry, chunk=chunk):
            for u in range(8):
                a = i * 8 + u
                early = recv_a[0, a].astype(f32)
                late = recv_a[1, a].astype(f32)
                if chunk == 0:
                    mine = jnp.where(low_lanes, early, late)
                else:
                    mine = pltpu.roll(jnp.where(low_lanes, late, early), 64, 1)
                gather[0, at(a * 32, 32), :] = mine
                gather[1, at(a * 32, 32), :] = recv_a[2 + chunk, a].astype(f32)
            return carry

        lax.fori_loop(0, DEVICES // 8, spread, 0)

        def pair_step(pair, carry, chunk=chunk):
            column_pair(
                pair, chunk, first_column, gather, (col_a, col_b, col_m, col_p),
                (col_twist, half_twist), edges, field,
            )
            return carry

        lax.fori_loop(0, 8, pair_step, 0)

        def pack_field(i, chunk=chunk):
            device = other(i)
            for part in range(2):
                send_c[chunk, device, part * 16 : part * 16 + 16, :] = field[
                    pl.ds(part * 128 + device, 16, stride=256), :
                ].astype(bf16)
            return device

        def send_field(i, chunk=chunk):
            device = pack_field(i)
            send(send_c.at[chunk, device], out.at[chunk, me], device, 5 + chunk)

        pack_field(0)
        keep(send_c.at[chunk, me], out.at[chunk, me], 5 + chunk)
        for i in range(1, 4):
            send_field(i)

        def field_step(i, carry, chunk=chunk):
            for u in range(4):
                send_field(i * 4 + u)
            return carry

        lax.fori_loop(1, DEVICES // 4, field_step, 0)

    for index in range(4):
        wait_send(send_a.at[index], index)
    wait_send(zones_out, 4)
    wait_recv(zones_out, 4)
    for chunk in range(2):
        wait_send(send_c.at[chunk], 5 + chunk)
        wait_recv(out.at[chunk], 5 + chunk)


def exchange(lobe_bounds, fringes, zones, tables):
    names = ("row_a", "row_twist", "row_b", "col_a", "col_b", "col_m", "col_p", "col_twist", "half_twist")
    constants = [tables[name] for name in names]
    return pl.pallas_call(
        spectrum_kernel,
        out_shape=(
            jax.ShapeDtypeStruct((2, DEVICES, 32, KEPT), bf16),
            jax.ShapeDtypeStruct((DEVICES, 1, 128), f32),
        ),
        in_specs=[
            pl.BlockSpec(memory_space=pltpu.SMEM),
            pl.BlockSpec(memory_space=pltpu.HBM),
            pl.BlockSpec(memory_space=pltpu.VMEM),
        ]
        + [pl.BlockSpec(memory_space=pltpu.HBM)] * len(names),
        out_specs=(pl.BlockSpec(memory_space=pltpu.HBM),) * 2,
        scratch_shapes=[pltpu.VMEM(value.shape, value.dtype) for value in constants]
        + [
            pltpu.VMEM((2, GROUP, W), bf16),
            pltpu.VMEM((2, 2, 16, 16 * GROUP, 128), bf16),
            pltpu.VMEM((32, 2, HALF, 128), bf16),
            pltpu.VMEM((4, DEVICES, 32, 128), bf16),
            pltpu.VMEM((4, DEVICES, 32, 128), bf16),
            pltpu.VMEM((2, DEVICES * 32, 128), f32),
            pltpu.VMEM((16 * 256, 128), f32),
            pltpu.VMEM((2, DEVICES, 32, KEPT), bf16),
            pltpu.VMEM((2, 1, 256), jnp.int32),
            pltpu.VMEM((8, 128), f32),
            pltpu.VMEM((1, 128), f32),
            pltpu.SemaphoreType.DMA((2,)),
            pltpu.SemaphoreType.DMA((7,)),
            pltpu.SemaphoreType.DMA((7,)),
            pltpu.SemaphoreType.DMA((7,)),
            pltpu.SemaphoreType.DMA((9,)),
        ],
        compiler_params=pltpu.CompilerParams(
            collective_id=0, has_side_effects=True, vmem_limit_bytes=60 << 20
        ),
        name="spectrum",
    )(lobe_bounds, fringes, zones, *constants)


def pixel_first(left, tile, half, pix_j, pix_twist, terms):
    mixed = dot(left, jnp.concatenate([pix_j[tile * 2], pix_j[tile * 2 + 1]], axis=1))
    for k0 in range(8):
        real = []
        imag = []
        for k1 in range(4):
            k = k1 * 8 + k0
            re = mixed[k * 16 : (k + 1) * 16, :128]
            im = mixed[k * 16 : (k + 1) * 16, 128:]
            if k:
                cosine = pix_twist[k, 0, tile]
                sine = pix_twist[k, 1, tile]
                cosine = jnp.concatenate([cosine, cosine], axis=0)
                sine = jnp.concatenate([sine, sine], axis=0)
                re, im = re * cosine - im * sine, im * cosine + re * sine
            real.append(re)
            imag.append(im)
        even_re, even_im = real[0] + real[2], imag[0] + imag[2]
        odd_re, odd_im = real[1] + real[3], imag[1] + imag[3]
        gap_re, gap_im = real[0] - real[2], imag[0] - imag[2]
        side_re, side_im = real[1] - real[3], imag[1] - imag[3]
        results = (
            (even_re + odd_re, even_im + odd_im),
            (gap_re - side_im, gap_im + side_re),
            (even_re - odd_re, even_im - odd_im),
            (gap_re + side_im, gap_im - side_re),
        )
        for p0 in range(4):
            for part in range(2):
                terms[p0, half, pl.ds(k0 * 32 + part * 16, 16), :] = results[p0][part].astype(bf16)


def pixel_second(group, q, pix_k, terms, zone_index, zone_table, pixels):
    for p0 in range(4):
        left = joined(pix_k.at[p0])
        mixed = [dot(left, joined(terms.at[u, p0])) for u in range(2)]
        for p1 in range(8):
            p = p0 + 4 * p1
            zone = zone_index[group, 2 * p + q // 2]
            source = lax.shift_right_logical(zone, 5)
            place = lax.bitwise_and(zone, 31)
            e0, e1, e2, e3 = (zone_table[source, place + 32 * r] for r in range(4))
            for u in range(2):
                real = mixed[u][p1 * 32 : p1 * 32 + 16]
                imag = mixed[u][p1 * 32 + 16 : p1 * 32 + 32]
                sine = imag * jnp.minimum(lax.rsqrt(real * real + imag * imag), 1.0 / damping_floor)
                heights = e0 + sine * (e1 + sine * (e2 + sine * e3))
                for h in range(2):
                    pixels[h * 8 : h * 8 + 8, pl.ds(1024 * p + (q + u) * 256, 256)] = heights[
                        h * 8 : h * 8 + 8
                    ].astype(bf16)


def height_kernel(
    zone_index, zone_table, received_in, pix_j_in, pix_twist_in, pix_k_in, out,
    received, pix_j, pix_twist, pix_k, rows, terms, pixels, store_sem, load_sem,
):
    loads = [
        pltpu.make_async_copy(source, target, load_sem.at[i])
        for i, (source, target) in enumerate(
            ((received_in, received), (pix_j_in, pix_j), (pix_twist_in, pix_twist), (pix_k_in, pix_k))
        )
    ]
    for copy in loads:
        copy.start()
    loads[0].wait()

    def flip(i, carry):
        for u in range(2):
            k = i * 2 + u
            for half in range(2):
                stacked = jnp.concatenate(
                    [
                        received[chunk, k * 4 + half * 2 + j]
                        for j in range(2)
                        for chunk in range(2)
                    ],
                    axis=0,
                )
                rows[k, half] = stacked.T
        return carry

    lax.fori_loop(0, 16, flip, 0)
    for copy in loads[1:]:
        copy.wait()
    groups = KEPT // ZB_R

    def store(group):
        slot = lax.rem(group, 2)
        return pltpu.make_async_copy(
            pixels.at[slot], out.at[at(group * ZB_R, ZB_R), :], store_sem.at[slot]
        )

    def front(group):
        left = jnp.concatenate(
            [rows[:, half, at(group * 16, 16), :].reshape(512, 128) for half in range(2)], axis=1
        )
        for q in range(4):
            for half in range(2):
                pixel_first(
                    left, q * 2 + half, half, pix_j, pix_twist, terms.at[lax.rem(group, 2), q]
                )

    def back(group):
        slot = lax.rem(group, 2)

        @pl.when(group >= 2)
        def _():
            store(group - 2).wait()

        for q in range(0, 4, 2):
            pixel_second(
                group, q, pix_k, terms.at[slot, pl.ds(q, 2)], zone_index, zone_table, pixels.at[slot]
            )

    front(0)

    def step(group, carry):
        back(group - 1)
        front(group)
        store(group - 1).start()
        return carry

    lax.fori_loop(1, groups, step, 0)
    back(groups - 1)
    store(groups - 1).start()
    store(groups - 2).wait()
    store(groups - 1).wait()


def height_map(zone_index, zone_table, received, tables):
    constants = [tables[name] for name in ("pix_j", "pix_twist", "pix_k")]
    return pl.pallas_call(
        height_kernel,
        out_shape=jax.ShapeDtypeStruct((KEPT, W), bf16),
        in_specs=[pl.BlockSpec(memory_space=pltpu.SMEM)] * 2
        + [pl.BlockSpec(memory_space=pltpu.HBM)] * 4,
        out_specs=pl.BlockSpec(memory_space=pltpu.HBM),
        scratch_shapes=[pltpu.VMEM(received.shape, received.dtype)]
        + [pltpu.VMEM(value.shape, value.dtype) for value in constants]
        + [
            pltpu.VMEM((32, 2, KEPT, 128), bf16),
            pltpu.VMEM((2, 4, 4, 2, 256, 128), bf16),
            pltpu.VMEM((2, ZB_R, W), bf16),
            pltpu.SemaphoreType.DMA((2,)),
            pltpu.SemaphoreType.DMA((4,)),
        ],
        compiler_params=pltpu.CompilerParams(vmem_limit_bytes=60 << 20),
        name="heights",
    )(zone_index, zone_table, received, *constants)


def body(tables, fringes, lobe_bounds, zone_index, zone_table):
    received, zones = exchange(lobe_bounds.T, fringes, zone_table, tables)
    return height_map(zone_index, zones.reshape(DEVICES, 128), received, tables)


def solution(mesh):
    placed = (P(("row", "col"), None), P(), P(("row", "col"), None), P(None, ("row", "col")))
    return jax.shard_map(
        functools.partial(body, make_tables()),
        mesh=mesh,
        in_specs=placed,
        out_specs=P(("row", "col"), None),
        check_vma=False,
    )
```

```python
import functools
import math

import jax
import jax.numpy as jnp
import ml_dtypes
import numpy as np
from jax import lax
from jax.experimental import pallas as pl
from jax.experimental.pallas import tpu as pltpu
from jax.sharding import PartitionSpec as P

W = 32768
H = 32768
LOBE = 4096
LOBE_START = 4096
DEVICES = 128
ROWS = H // DEVICES
HALF = ROWS // 2
KEPT = H // (2 * DEVICES)
GROUP = 32
COLUMNS = 4
ZB_R = 16

damping_floor = 0.5
bf16 = jnp.bfloat16
f32 = jnp.float32
MESH = pl.DeviceIdType.MESH


def turns(first, second, period):
    angles = (np.outer(first, second) % period).astype(np.float64) * (2.0 * math.pi / period)
    return np.cos(angles), np.sin(angles)


def lane_tiles(matrix):
    shape = matrix.shape
    return np.moveaxis(matrix.reshape(*shape[:-1], shape[-1] // 128, 128), -2, -3)


def by_tile(rows):
    first, two, length = rows.shape
    return np.broadcast_to(
        rows.reshape(first, two, length // 128, 1, 128), (first, two, length // 128, 8, 128)
    )


def make_tables():
    n4, n8, n16, n32 = (np.arange(n) for n in (4, 8, 16, 32))
    n128, n256, n1024, n2048 = (np.arange(n) for n in (128, 256, 1024, 2048))
    half = {}
    full = {}
    cosine, sine = turns(n16, n16, 16)
    half["row_a"] = np.kron(np.concatenate([cosine[:9], -sine[1:8]], 0), np.eye(16))
    cosine, sine = turns(n16, n2048, W)
    full["row_twist"] = by_tile(np.stack([cosine, sine], 1))
    sides = []
    for odd in range(2):
        cosine, sine = turns(n1024, LOBE_START // 16 + 2 * n128 + odd, 2048)
        real = np.concatenate([cosine, sine], 0).reshape(2048, 4, 2, 16)
        imag = np.concatenate([-sine, cosine], 0).reshape(2048, 4, 2, 16)
        sides.append(np.stack([real, imag], 3).transpose(0, 2, 1, 3, 4).reshape(2048, 256))
    half["row_b"] = np.stack(sides)
    cosine, sine = turns(n128, n128, 128)
    half["col_a"] = np.block([[cosine, sine], [-sine, cosine]])
    half["col_m"] = np.block([[cosine, sine], [-sine, cosine]])
    half["col_p"] = np.block([[cosine, -sine], [sine, cosine]])
    cosine, sine = turns(n128, n256, H)
    full["col_twist"] = np.stack([cosine, sine])
    cosine, sine = turns(n256, n256, 256)
    half["col_b"] = np.block([[cosine, -sine], [sine, cosine]])
    cosine, sine = turns(n128, n128, H // 2)
    full["half_twist"] = np.stack([cosine, sine])
    cosine, sine = turns(n128, n1024, 1024)
    real = np.stack([cosine.reshape(128, 8, 128), sine.reshape(128, 8, 128)], 2).reshape(128, 2048)
    imag = np.stack([-sine.reshape(128, 8, 128), cosine.reshape(128, 8, 128)], 2).reshape(128, 2048)
    half["pix_j"] = np.stack([real.reshape(4, 2, 16, 2048), imag.reshape(4, 2, 16, 2048)], 2).reshape(
        256, 2048
    )
    cosine, sine = turns(n32, n1024, W)
    full["pix_twist"] = by_tile(np.stack([cosine, sine], 1))
    mats = []
    for p0 in range(4):
        cosine, sine = turns(p0 + 4 * n8, n8, 32)
        block = np.stack(
            [np.stack([cosine, -sine], -1), np.stack([sine, cosine], -1)], 1
        ).reshape(16, 16)
        mats.append(np.kron(block, np.eye(16)))
    half["pix_k"] = np.stack(mats)
    made = {name: lane_tiles(value).astype(ml_dtypes.bfloat16) for name, value in half.items()}
    made.update({name: np.ascontiguousarray(value, np.float32) for name, value in full.items()})
    return made


def dot(left, right):
    return jnp.dot(left, right, preferred_element_type=f32)


def joined(tiles):
    return jnp.concatenate([tiles[i] for i in range(tiles.shape[0])], axis=1)


def at(start, size):
    return pl.ds(pl.multiple_of(start, size), size)


def row_first(block, pair, rows16, mat, twist, mid):
    sides = [
        [
            block[pl.ds(rows16 * 16, 16), at(2048 * a + 1024 * upper + pair * 256, 256)]
            for a in range(16)
        ]
        for upper in range(2)
    ]
    left = joined(mat)
    rows = [pl.ds(k * GROUP + rows16 * 16, 16) for k in range(16)]
    for v in range(2):
        tile = pair * 2 + v
        right = jnp.concatenate(
            [
                jnp.concatenate([piece[:, v * 128 : v * 128 + 128] for piece in side], axis=0)
                for side in sides
            ],
            axis=1,
        )
        mixed = dot(left, right)

        def part(index, upper):
            return mixed[index * 16 : (index + 1) * 16, upper * 128 : (upper + 1) * 128]

        def factor(k, index, upper):
            value = twist[k, index, upper * 8 + tile]
            return jnp.concatenate([value, value], axis=0)

        for k in range(16):
            twisted = []
            for upper in range(2):
                source = k if k <= 8 else 16 - k
                real = part(source, upper)
                if k == 0:
                    twisted.append((real, None))
                    continue
                cosine = factor(k, 0, upper)
                sine = factor(k, 1, upper)
                if k == 8:
                    twisted.append((real * cosine, -(real * sine)))
                    continue
                imag = part(source + 8, upper)
                if k < 8:
                    twisted.append((real * cosine + imag * sine, imag * cosine - real * sine))
                else:
                    twisted.append((real * cosine - imag * sine, -(imag * cosine + real * sine)))
            (real0, imag0), (real1, imag1) = twisted
            mid[0, tile, rows[k], :] = (real0 + real1).astype(bf16)
            mid[1, tile, rows[k], :] = (real0 - real1).astype(bf16)
            if imag0 is None:
                mid[0, 8 + tile, rows[k], :] = jnp.zeros((16, 128), bf16)
                mid[1, 8 + tile, rows[k], :] = jnp.zeros((16, 128), bf16)
            else:
                mid[0, 8 + tile, rows[k], :] = (imag0 + imag1).astype(bf16)
                mid[1, 8 + tile, rows[k], :] = (imag0 - imag1).astype(bf16)


def row_second(mid, odd, block, mat, lobe, group):
    rows = 8 * GROUP
    left = jnp.concatenate([mid[odd, t, at(block * rows, rows), :] for t in range(16)], axis=1)
    mixed = dot(left, joined(mat.at[odd])).astype(bf16)
    for k in range(8):
        for chunk in range(2):
            lobe[odd * 16 + block * 8 + k, chunk, at(group * GROUP, GROUP), :] = mixed[
                k * GROUP : (k + 1) * GROUP, chunk * 128 : chunk * 128 + 128
            ]


def column_set(index, chunk, first_column, gather, mats, twists, edges, field):
    col_a, col_b, col_m, col_p = mats
    col_twist, half_twist = twists
    inputs = []
    for u in range(COLUMNS):
        j = index * COLUMNS + u
        parts = []
        for part in range(2):
            parts.append(
                jnp.concatenate(
                    [gather[h, pl.ds(part * 16 + j, DEVICES, stride=32), :] for h in range(2)],
                    axis=1,
                )
            )
        inputs.append(jnp.concatenate(parts, axis=0).astype(bf16))
    mixed = dot(joined(col_a), jnp.concatenate(inputs, axis=1))
    middles = []
    for u in range(COLUMNS):
        lanes = slice(u * 256, (u + 1) * 256)
        real, imag = mixed[:128, lanes], mixed[128:, lanes]
        cosine, sine = col_twist[0], col_twist[1]
        middles.append(
            jnp.concatenate(
                [
                    (real * cosine + imag * sine).astype(bf16),
                    (imag * cosine - real * sine).astype(bf16),
                ],
                axis=1,
            )
        )
    spectrum = dot(jnp.concatenate(middles, axis=0), joined(col_b))
    folded = []
    for u in range(COLUMNS):
        column = first_column + 32 * (chunk * 16 + index * COLUMNS + u)
        keep = jnp.where((column >= edges[0]) & (column < edges[1]), 1.0 / (H * W), 0.0)
        rows = spectrum[u * 128 : (u + 1) * 128]
        folded.append(
            jnp.concatenate(
                [
                    (
                        rows[:, part * 256 : part * 256 + 128] * keep[:, :128]
                        + rows[:, part * 256 + 128 : part * 256 + 256] * keep[:, 128:]
                    ).astype(bf16)
                    for part in range(2)
                ],
                axis=1,
            )
        )
    halves = dot(jnp.concatenate(folded, axis=0), joined(col_m))
    cosine, sine = half_twist[0], half_twist[1]
    terms = []
    for u in range(COLUMNS):
        rows = halves[u * 128 : (u + 1) * 128]
        real, imag = rows[:, :128], rows[:, 128:]
        terms.append(
            jnp.concatenate(
                [
                    (real * cosine - imag * sine).astype(bf16),
                    (imag * cosine + real * sine).astype(bf16),
                ],
                axis=0,
            )
        )
    out = dot(joined(col_p), jnp.concatenate(terms, axis=1))
    for u in range(COLUMNS):
        field[at((index * COLUMNS + u) * 256, 256), :] = out[:, u * 128 : (u + 1) * 128]


def spectrum_kernel(
    bounds, fringes, zones, *refs,
):
    given, refs = refs[:9], refs[9:]
    out, zones_out, *refs = refs
    tables, refs = refs[:9], refs[9:]
    row_a, row_twist, row_b, col_a, col_b, col_m, col_p, col_twist, half_twist = tables
    block, mid, lobe, send_a, recv_a, gather, field, send_c, edges, zone_rows, zone_row = refs[:11]
    load_sem, send_sem, recv_sem, own_sem, table_sem = refs[11:]
    table_copies = [
        pltpu.make_async_copy(given[i], tables[i], table_sem.at[i]) for i in range(9)
    ]
    my_row = lax.axis_index("row")
    my_col = lax.axis_index("col")
    cols = lax.axis_size("col")
    me = my_row * cols + my_col

    def place(device):
        return (lax.div(device, cols), lax.rem(device, cols))

    def other(i):
        return lax.rem(me + i, DEVICES)

    barrier = pltpu.get_barrier_semaphore()

    def greet(i, carry):
        pl.semaphore_signal(barrier, inc=1, device_id=place(other(i)), device_id_type=MESH)
        return carry

    def load(group, slot):
        return pltpu.make_async_copy(
            fringes.at[at(group * GROUP, GROUP), :], block.at[slot], load_sem.at[slot]
        )

    def send(source, target, device, index):
        pltpu.make_async_remote_copy(
            src_ref=source, dst_ref=target, send_sem=send_sem.at[index],
            recv_sem=recv_sem.at[index], device_id=place(device), device_id_type=MESH,
        ).start()

    def keep(source, target, index):
        pltpu.make_async_copy(source, target, own_sem.at[index]).start()

    def wait_recv(buffer, index):
        others = buffer.at[pl.ds(0, DEVICES - 1)]
        pltpu.make_async_copy(others, others, recv_sem.at[index]).wait()
        pltpu.make_async_copy(buffer.at[0], buffer.at[0], own_sem.at[index]).wait()

    def wait_send(buffer, index):
        others = buffer.at[pl.ds(0, DEVICES - 1)]
        pltpu.make_async_copy(others, others, send_sem.at[index]).wait()

    load(0, 0).start()
    for copy in table_copies:
        copy.start()
    lax.fori_loop(1, DEVICES, greet, 0)

    lanes = lax.broadcasted_iota(jnp.int32, (1, 256), 1)

    def edge_step(t, carry):
        mine = (lanes >= 4 * t) & (lanes < 4 * t + 4)
        return tuple(jnp.where(mine, bounds[side, t], carry[side]) for side in range(2))

    both = lax.fori_loop(0, 64, edge_step, (jnp.zeros((1, 256), jnp.int32),) * 2)
    edges[0] = both[0]
    edges[1] = both[1]
    zone_rows[...] = jnp.zeros((8, 128), f32)
    zone_rows[0:4, 0:32] = zones[...]
    spread_rows = zone_rows[...]
    zone_row[...] = spread_rows[0:1] + sum(
        pltpu.roll(spread_rows, 32 * r, 1)[r : r + 1] for r in range(1, 4)
    )

    table_copies[0].wait()
    table_copies[1].wait()

    def first_only(group):
        slot = lax.rem(group, 2)
        load(group + 1, 1 - slot).start()
        load(group, slot).wait()

        def piece(pair, carry):
            for rows16 in range(2):
                row_first(block.at[slot], pair, rows16, row_a, row_twist, mid.at[slot])
            return carry

        lax.fori_loop(0, 4, piece, 0)

    def both_steps(group, last):
        slot = lax.rem(group, 2)
        if not last:
            load(group + 1, 1 - slot).start()
        load(group, slot).wait()

        def piece(i, carry):
            row_second(
                mid.at[1 - slot], lax.div(i, 2), lax.rem(i, 2), row_b, lobe, lax.rem(group - 1, 4)
            )
            for rows16 in range(2):
                row_first(block.at[slot], i, rows16, row_a, row_twist, mid.at[slot])
            return carry

        lax.fori_loop(0, 4, piece, 0)

    def second_only(group):
        slot = lax.rem(group, 2)

        def piece(i, carry):
            row_second(mid.at[slot], lax.div(i, 2), lax.rem(i, 2), row_b, lobe, lax.rem(group, 4))
            return carry

        lax.fori_loop(0, 4, piece, 0)

    def send_block(buffer, target, k, low, index):
        for j in range(low, 4):
            device = k * 4 + lax.rem(me + j, 4)
            send(buffer.at[device], target.at[me], device, index)

    def quarter_step(c, carry):
        first_only(2 * c)

        @pl.when(c == 0)
        def _():
            table_copies[2].wait()

        both_steps(2 * c + 1, False)
        second_only(2 * c + 1)

        @pl.when(c == 0)
        def _():
            pl.semaphore_wait(barrier, DEVICES - 1)

        def pack(i):
            k = lax.rem(lax.div(me, 4) + i, 32)
            rows = at(c * 64, 64)
            upper = lobe[k, c, rows, :]
            lower = lobe[k, 1 - c, rows, :]
            flipped = jnp.concatenate([upper, lower], axis=0).T
            for j in range(4):
                send_a[c, k * 4 + j] = flipped[j * 32 : (j + 1) * 32]
            return k

        k = pack(0)
        keep(send_a.at[c, me], recv_a.at[c, me], c)
        send_block(send_a.at[c], recv_a.at[c], k, 1, c)

        def pack_step(i, inner):
            send_block(send_a.at[c], recv_a.at[c], pack(i), 0, c)
            return inner

        lax.fori_loop(1, 32, pack_step, 0)
        return carry

    lax.fori_loop(0, 2, quarter_step, 0)

    keep(zone_row, zones_out.at[me], 4)

    def send_zones(i, carry):
        send(zone_row, zones_out.at[me], other(i), 4)
        return carry

    first_only(4)

    def half_step(g, carry):
        both_steps(g, False)
        return carry

    lax.fori_loop(5, 7, half_step, 0)
    both_steps(7, True)
    second_only(7)

    def pack_half(i):
        k = lax.rem(lax.div(me, 4) + i, 32)
        for chunk in range(2):
            flipped = lobe[k, chunk].T
            for j in range(4):
                send_a[2 + chunk, k * 4 + j] = flipped[j * 32 : (j + 1) * 32]
        return k

    k = pack_half(0)
    keep(send_a.at[2, me], recv_a.at[2, me], 2)
    send_block(send_a.at[2], recv_a.at[2], k, 1, 2)

    def pack_half_step(i, carry):
        send_block(send_a.at[2], recv_a.at[2], pack_half(i), 0, 2)
        return carry

    lax.fori_loop(1, 32, pack_half_step, 0)
    keep(send_a.at[3, me], recv_a.at[3, me], 3)

    def send_last(i, carry):
        send(send_a.at[3, other(i)], recv_a.at[3, me], other(i), 3)
        return carry

    lax.fori_loop(1, DEVICES, send_last, 0)
    lax.fori_loop(1, DEVICES, send_zones, 0)

    first_column = lax.div(me, 4) + 32 * 32 * lax.rem(me, 4)
    low_lanes = lax.broadcasted_iota(jnp.int32, (32, 128), 1) < 64
    for copy in table_copies[3:]:
        copy.wait()
    wait_recv(recv_a.at[0], 0)
    wait_recv(recv_a.at[1], 1)
    for chunk in range(2):
        wait_recv(recv_a.at[2 + chunk], 2 + chunk)

        def spread(i, carry, chunk=chunk):
            for u in range(8):
                a = i * 8 + u
                early = recv_a[0, a].astype(f32)
                late = recv_a[1, a].astype(f32)
                if chunk == 0:
                    mine = jnp.where(low_lanes, early, late)
                else:
                    mine = pltpu.roll(jnp.where(low_lanes, late, early), 64, 1)
                gather[0, at(a * 32, 32), :] = mine
                gather[1, at(a * 32, 32), :] = recv_a[2 + chunk, a].astype(f32)
            return carry

        lax.fori_loop(0, DEVICES // 8, spread, 0)

        def column_step(index, carry, chunk=chunk):
            column_set(
                index, chunk, first_column, gather, (col_a, col_b, col_m, col_p),
                (col_twist, half_twist), edges, field,
            )
            return carry

        lax.fori_loop(0, 16 // COLUMNS, column_step, 0)

        def pack_field(i, chunk=chunk):
            device = other(i)
            for part in range(2):
                send_c[chunk, device, part * 16 : part * 16 + 16, :] = field[
                    pl.ds(part * 128 + device, 16, stride=256), :
                ].astype(bf16)
            return device

        def send_field(i, chunk=chunk):
            device = pack_field(i)
            send(send_c.at[chunk, device], out.at[chunk, me], device, 5 + chunk)

        pack_field(0)
        keep(send_c.at[chunk, me], out.at[chunk, me], 5 + chunk)
        for i in range(1, 4):
            send_field(i)

        def field_step(i, carry, chunk=chunk):
            for u in range(4):
                send_field(i * 4 + u)
            return carry

        lax.fori_loop(1, DEVICES // 4, field_step, 0)

    for index in range(4):
        wait_send(send_a.at[index], index)
    wait_send(zones_out, 4)
    wait_recv(zones_out, 4)
    for chunk in range(2):
        wait_send(send_c.at[chunk], 5 + chunk)
        wait_recv(out.at[chunk], 5 + chunk)


def exchange(lobe_bounds, fringes, zones, tables):
    names = ("row_a", "row_twist", "row_b", "col_a", "col_b", "col_m", "col_p", "col_twist", "half_twist")
    constants = [tables[name] for name in names]
    return pl.pallas_call(
        spectrum_kernel,
        out_shape=(
            jax.ShapeDtypeStruct((2, DEVICES, 32, KEPT), bf16),
            jax.ShapeDtypeStruct((DEVICES, 1, 128), f32),
        ),
        in_specs=[
            pl.BlockSpec(memory_space=pltpu.SMEM),
            pl.BlockSpec(memory_space=pltpu.HBM),
            pl.BlockSpec(memory_space=pltpu.VMEM),
        ]
        + [pl.BlockSpec(memory_space=pltpu.HBM)] * len(names),
        out_specs=(pl.BlockSpec(memory_space=pltpu.HBM),) * 2,
        scratch_shapes=[pltpu.VMEM(value.shape, value.dtype) for value in constants]
        + [
            pltpu.VMEM((2, GROUP, W), bf16),
            pltpu.VMEM((2, 2, 16, 16 * GROUP, 128), bf16),
            pltpu.VMEM((32, 2, HALF, 128), bf16),
            pltpu.VMEM((4, DEVICES, 32, 128), bf16),
            pltpu.VMEM((4, DEVICES, 32, 128), bf16),
            pltpu.VMEM((2, DEVICES * 32, 128), f32),
            pltpu.VMEM((16 * 256, 128), f32),
            pltpu.VMEM((2, DEVICES, 32, KEPT), bf16),
            pltpu.VMEM((2, 1, 256), jnp.int32),
            pltpu.VMEM((8, 128), f32),
            pltpu.VMEM((1, 128), f32),
            pltpu.SemaphoreType.DMA((2,)),
            pltpu.SemaphoreType.DMA((7,)),
            pltpu.SemaphoreType.DMA((7,)),
            pltpu.SemaphoreType.DMA((7,)),
            pltpu.SemaphoreType.DMA((9,)),
        ],
        compiler_params=pltpu.CompilerParams(
            collective_id=0, has_side_effects=True, vmem_limit_bytes=60 << 20
        ),
        name="spectrum",
    )(lobe_bounds, fringes, zones, *constants)


def pixel_first(left, tile, half, pix_j, pix_twist, terms):
    mixed = dot(left, jnp.concatenate([pix_j[tile * 2], pix_j[tile * 2 + 1]], axis=1))
    for k0 in range(8):
        real = []
        imag = []
        for k1 in range(4):
            k = k1 * 8 + k0
            re = mixed[k * 16 : (k + 1) * 16, :128]
            im = mixed[k * 16 : (k + 1) * 16, 128:]
            if k:
                cosine = pix_twist[k, 0, tile]
                sine = pix_twist[k, 1, tile]
                cosine = jnp.concatenate([cosine, cosine], axis=0)
                sine = jnp.concatenate([sine, sine], axis=0)
                re, im = re * cosine - im * sine, im * cosine + re * sine
            real.append(re)
            imag.append(im)
        even_re, even_im = real[0] + real[2], imag[0] + imag[2]
        odd_re, odd_im = real[1] + real[3], imag[1] + imag[3]
        gap_re, gap_im = real[0] - real[2], imag[0] - imag[2]
        side_re, side_im = real[1] - real[3], imag[1] - imag[3]
        results = (
            (even_re + odd_re, even_im + odd_im),
            (gap_re - side_im, gap_im + side_re),
            (even_re - odd_re, even_im - odd_im),
            (gap_re + side_im, gap_im - side_re),
        )
        for p0 in range(4):
            for part in range(2):
                terms[p0, half, pl.ds(k0 * 32 + part * 16, 16), :] = results[p0][part].astype(bf16)


def pixel_second(group, q, pix_k, terms, zone_index, zone_table, pixels):
    for p0 in range(4):
        left = joined(pix_k.at[p0])
        mixed = [dot(left, joined(terms.at[u, p0])) for u in range(2)]
        for p1 in range(8):
            p = p0 + 4 * p1
            zone = zone_index[group, 2 * p + q // 2]
            source = lax.shift_right_logical(zone, 5)
            place = lax.bitwise_and(zone, 31)
            e0, e1, e2, e3 = (zone_table[source, place + 32 * r] for r in range(4))
            for u in range(2):
                real = mixed[u][p1 * 32 : p1 * 32 + 16]
                imag = mixed[u][p1 * 32 + 16 : p1 * 32 + 32]
                sine = imag * jnp.minimum(lax.rsqrt(real * real + imag * imag), 1.0 / damping_floor)
                heights = e0 + sine * (e1 + sine * (e2 + sine * e3))
                for h in range(2):
                    pixels[h * 8 : h * 8 + 8, pl.ds(1024 * p + (q + u) * 256, 256)] = heights[
                        h * 8 : h * 8 + 8
                    ].astype(bf16)


def height_kernel(
    zone_index, zone_table, received_in, pix_j_in, pix_twist_in, pix_k_in, out,
    received, pix_j, pix_twist, pix_k, rows, terms, pixels, store_sem, load_sem,
):
    loads = [
        pltpu.make_async_copy(source, target, load_sem.at[i])
        for i, (source, target) in enumerate(
            ((received_in, received), (pix_j_in, pix_j), (pix_twist_in, pix_twist), (pix_k_in, pix_k))
        )
    ]
    for copy in loads:
        copy.start()
    loads[0].wait()

    def flip(i, carry):
        for u in range(2):
            k = i * 2 + u
            for half in range(2):
                stacked = jnp.concatenate(
                    [
                        received[chunk, k * 4 + half * 2 + j]
                        for j in range(2)
                        for chunk in range(2)
                    ],
                    axis=0,
                )
                rows[k, half] = stacked.T
        return carry

    lax.fori_loop(0, 16, flip, 0)
    for copy in loads[1:]:
        copy.wait()
    groups = KEPT // ZB_R

    def store(group):
        slot = lax.rem(group, 2)
        return pltpu.make_async_copy(
            pixels.at[slot], out.at[at(group * ZB_R, ZB_R), :], store_sem.at[slot]
        )

    def front(group):
        left = jnp.concatenate(
            [rows[:, half, at(group * 16, 16), :].reshape(512, 128) for half in range(2)], axis=1
        )
        for q in range(4):
            for half in range(2):
                pixel_first(
                    left, q * 2 + half, half, pix_j, pix_twist, terms.at[lax.rem(group, 2), q]
                )

    def back(group):
        slot = lax.rem(group, 2)

        @pl.when(group >= 2)
        def _():
            store(group - 2).wait()

        for q in range(0, 4, 2):
            pixel_second(
                group, q, pix_k, terms.at[slot, pl.ds(q, 2)], zone_index, zone_table, pixels.at[slot]
            )

    front(0)

    def step(group, carry):
        back(group - 1)
        front(group)
        store(group - 1).start()
        return carry

    lax.fori_loop(1, groups, step, 0)
    back(groups - 1)
    store(groups - 1).start()
    store(groups - 2).wait()
    store(groups - 1).wait()


def height_map(zone_index, zone_table, received, tables):
    constants = [tables[name] for name in ("pix_j", "pix_twist", "pix_k")]
    return pl.pallas_call(
        height_kernel,
        out_shape=jax.ShapeDtypeStruct((KEPT, W), bf16),
        in_specs=[pl.BlockSpec(memory_space=pltpu.SMEM)] * 2
        + [pl.BlockSpec(memory_space=pltpu.HBM)] * 4,
        out_specs=pl.BlockSpec(memory_space=pltpu.HBM),
        scratch_shapes=[pltpu.VMEM(received.shape, received.dtype)]
        + [pltpu.VMEM(value.shape, value.dtype) for value in constants]
        + [
            pltpu.VMEM((32, 2, KEPT, 128), bf16),
            pltpu.VMEM((2, 4, 4, 2, 256, 128), bf16),
            pltpu.VMEM((2, ZB_R, W), bf16),
            pltpu.SemaphoreType.DMA((2,)),
            pltpu.SemaphoreType.DMA((4,)),
        ],
        compiler_params=pltpu.CompilerParams(vmem_limit_bytes=60 << 20),
        name="heights",
    )(zone_index, zone_table, received, *constants)


def body(tables, fringes, lobe_bounds, zone_index, zone_table):
    received, zones = exchange(lobe_bounds.T, fringes, zone_table, tables)
    return height_map(zone_index, zones.reshape(DEVICES, 128), received, tables)


def solution(mesh):
    placed = (P(("row", "col"), None), P(), P(("row", "col"), None), P(None, ("row", "col")))
    return jax.shard_map(
        functools.partial(body, make_tables()),
        mesh=mesh,
        in_specs=placed,
        out_specs=P(("row", "col"), None),
        check_vma=False,
    )
```

```python
import functools
import math

import jax
import jax.numpy as jnp
import ml_dtypes
import numpy as np
from jax import lax
from jax.experimental import pallas as pl
from jax.experimental.pallas import tpu as pltpu
from jax.sharding import PartitionSpec as P

W = 32768
H = 32768
LOBE = 4096
LOBE_START = 4096
DEVICES = 128
ROWS = H // DEVICES
HALF = ROWS // 2
KEPT = H // (2 * DEVICES)
GROUP = 32
COLUMNS = 4
ZB_R = 16

damping_floor = 0.5
bf16 = jnp.bfloat16
f32 = jnp.float32
MESH = pl.DeviceIdType.MESH


def turns(first, second, period):
    angles = (np.outer(first, second) % period).astype(np.float64) * (2.0 * math.pi / period)
    return np.cos(angles), np.sin(angles)


def lane_tiles(matrix):
    shape = matrix.shape
    return np.moveaxis(matrix.reshape(*shape[:-1], shape[-1] // 128, 128), -2, -3)


def by_tile(rows):
    first, two, length = rows.shape
    return np.broadcast_to(
        rows.reshape(first, two, length // 128, 1, 128), (first, two, length // 128, 8, 128)
    )


def make_tables():
    n4, n8, n16, n32 = (np.arange(n) for n in (4, 8, 16, 32))
    n128, n256, n1024, n2048 = (np.arange(n) for n in (128, 256, 1024, 2048))
    half = {}
    full = {}
    cosine, sine = turns(n16, n16, 16)
    half["row_a"] = np.kron(np.concatenate([cosine[:9], -sine[1:8]], 0), np.eye(16))
    cosine, sine = turns(n16, n2048, W)
    full["row_twist"] = np.stack([cosine, sine], 1).reshape(512, 128)
    sides = []
    for odd in range(2):
        cosine, sine = turns(n1024, LOBE_START // 16 + 2 * n128 + odd, 2048)
        real = np.concatenate([cosine, sine], 0).reshape(2048, 4, 2, 16)
        imag = np.concatenate([-sine, cosine], 0).reshape(2048, 4, 2, 16)
        sides.append(np.stack([real, imag], 3).transpose(0, 2, 1, 3, 4).reshape(2048, 256))
    half["row_b"] = np.stack(sides)
    cosine, sine = turns(n128, n128, 128)
    half["col_a"] = np.block([[cosine, sine], [-sine, cosine]])
    half["col_m"] = np.block([[cosine, sine], [-sine, cosine]])
    half["col_p"] = np.block([[cosine, -sine], [sine, cosine]])
    cosine, sine = turns(n128, n256, H)
    full["col_twist"] = np.stack([cosine, sine])
    cosine, sine = turns(n256, n256, 256)
    half["col_b"] = np.block([[cosine, -sine], [sine, cosine]])
    cosine, sine = turns(n128, n128, H // 2)
    full["half_twist"] = np.stack([cosine, sine])
    cosine, sine = turns(n128, n1024, 1024)
    real = np.stack([cosine.reshape(128, 8, 128), sine.reshape(128, 8, 128)], 2).reshape(128, 2048)
    imag = np.stack([-sine.reshape(128, 8, 128), cosine.reshape(128, 8, 128)], 2).reshape(128, 2048)
    half["pix_j"] = np.stack([real.reshape(4, 2, 16, 2048), imag.reshape(4, 2, 16, 2048)], 2).reshape(
        256, 2048
    )
    cosine, sine = turns(n32, n1024, W)
    full["pix_twist"] = by_tile(np.stack([cosine, sine], 1))
    mats = []
    for p0 in range(4):
        cosine, sine = turns(p0 + 4 * n8, n8, 32)
        block = np.stack(
            [np.stack([cosine, -sine], -1), np.stack([sine, cosine], -1)], 1
        ).reshape(16, 16)
        mats.append(np.kron(block, np.eye(16)))
    half["pix_k"] = np.stack(mats)
    made = {name: lane_tiles(value).astype(ml_dtypes.bfloat16) for name, value in half.items()}
    made.update({name: np.ascontiguousarray(value, np.float32) for name, value in full.items()})
    return made


def dot(left, right):
    return jnp.dot(left, right, preferred_element_type=f32)


def joined(tiles):
    return jnp.concatenate([tiles[i] for i in range(tiles.shape[0])], axis=1)


def at(start, size):
    return pl.ds(pl.multiple_of(start, size), size)


def row_first(block, pair, rows16, mat, twist, mid):
    sides = [
        [
            block[pl.ds(rows16 * 16, 16), at(2048 * a + 1024 * upper + pair * 256, 256)]
            for a in range(16)
        ]
        for upper in range(2)
    ]
    left = joined(mat)
    rows = [pl.ds(k * GROUP + rows16 * 16, 16) for k in range(16)]
    for v in range(2):
        tile = pair * 2 + v
        right = jnp.concatenate(
            [
                jnp.concatenate([piece[:, v * 128 : v * 128 + 128] for piece in side], axis=0)
                for side in sides
            ],
            axis=1,
        )
        mixed = dot(left, right)

        def part(index, upper):
            return mixed[index * 16 : (index + 1) * 16, upper * 128 : (upper + 1) * 128]

        def factor(k, index, upper):
            value = twist[(k * 2 + index) * 16 + upper * 8 + tile]
            return jnp.concatenate([value, value], axis=0)

        for k in range(16):
            twisted = []
            for upper in range(2):
                source = k if k <= 8 else 16 - k
                real = part(source, upper)
                if k == 0:
                    twisted.append((real, None))
                    continue
                cosine = factor(k, 0, upper)
                sine = factor(k, 1, upper)
                if k == 8:
                    twisted.append((real * cosine, -(real * sine)))
                    continue
                imag = part(source + 8, upper)
                if k < 8:
                    twisted.append((real * cosine + imag * sine, imag * cosine - real * sine))
                else:
                    twisted.append((real * cosine - imag * sine, -(imag * cosine + real * sine)))
            (real0, imag0), (real1, imag1) = twisted
            mid[0, tile, rows[k], :] = (real0 + real1).astype(bf16)
            mid[1, tile, rows[k], :] = (real0 - real1).astype(bf16)
            if imag0 is None:
                mid[0, 8 + tile, rows[k], :] = jnp.zeros((16, 128), bf16)
                mid[1, 8 + tile, rows[k], :] = jnp.zeros((16, 128), bf16)
            else:
                mid[0, 8 + tile, rows[k], :] = (imag0 + imag1).astype(bf16)
                mid[1, 8 + tile, rows[k], :] = (imag0 - imag1).astype(bf16)


def row_second(mid, odd, block, mat, lobe, group):
    rows = 8 * GROUP
    left = jnp.concatenate([mid[odd, t, at(block * rows, rows), :] for t in range(16)], axis=1)
    mixed = dot(left, joined(mat.at[odd])).astype(bf16)
    for k in range(8):
        for chunk in range(2):
            lobe[odd * 16 + block * 8 + k, chunk, at(group * GROUP, GROUP), :] = mixed[
                k * GROUP : (k + 1) * GROUP, chunk * 128 : chunk * 128 + 128
            ]


def column_set(index, chunk, first_column, gather, mats, twists, edges, field):
    col_a, col_b, col_m, col_p = mats
    col_twist, half_twist = twists
    inputs = []
    for u in range(COLUMNS):
        j = index * COLUMNS + u
        parts = []
        for part in range(2):
            parts.append(
                jnp.concatenate(
                    [gather[h, pl.ds(part * 16 + j, DEVICES, stride=32), :] for h in range(2)],
                    axis=1,
                )
            )
        inputs.append(jnp.concatenate(parts, axis=0).astype(bf16))
    mixed = dot(joined(col_a), jnp.concatenate(inputs, axis=1))
    middles = []
    for u in range(COLUMNS):
        lanes = slice(u * 256, (u + 1) * 256)
        real, imag = mixed[:128, lanes], mixed[128:, lanes]
        cosine, sine = col_twist[0], col_twist[1]
        middles.append(
            jnp.concatenate(
                [
                    (real * cosine + imag * sine).astype(bf16),
                    (imag * cosine - real * sine).astype(bf16),
                ],
                axis=1,
            )
        )
    spectrum = dot(jnp.concatenate(middles, axis=0), joined(col_b))
    folded = []
    for u in range(COLUMNS):
        column = first_column + 32 * (chunk * 16 + index * COLUMNS + u)
        keep = jnp.where((column >= edges[0]) & (column < edges[1]), 1.0 / (H * W), 0.0)
        rows = spectrum[u * 128 : (u + 1) * 128]
        folded.append(
            jnp.concatenate(
                [
                    (
                        rows[:, part * 256 : part * 256 + 128] * keep[:, :128]
                        + rows[:, part * 256 + 128 : part * 256 + 256] * keep[:, 128:]
                    ).astype(bf16)
                    for part in range(2)
                ],
                axis=1,
            )
        )
    halves = dot(jnp.concatenate(folded, axis=0), joined(col_m))
    cosine, sine = half_twist[0], half_twist[1]
    terms = []
    for u in range(COLUMNS):
        rows = halves[u * 128 : (u + 1) * 128]
        real, imag = rows[:, :128], rows[:, 128:]
        terms.append(
            jnp.concatenate(
                [
                    (real * cosine - imag * sine).astype(bf16),
                    (imag * cosine + real * sine).astype(bf16),
                ],
                axis=0,
            )
        )
    out = dot(joined(col_p), jnp.concatenate(terms, axis=1))
    for u in range(COLUMNS):
        field[at((index * COLUMNS + u) * 256, 256), :] = out[:, u * 128 : (u + 1) * 128]


def spectrum_kernel(
    bounds, fringes, zones, *refs,
):
    given, refs = refs[:9], refs[9:]
    out, zones_out, *refs = refs
    tables, refs = refs[:9], refs[9:]
    row_a, row_twist, row_b, col_a, col_b, col_m, col_p, col_twist, half_twist = tables
    block, mid, lobe, send_a, recv_a, gather, field, send_c, edges, zone_rows, zone_row, twists = refs[:12]
    load_sem, send_sem, recv_sem, own_sem, table_sem = refs[12:]
    table_copies = [
        pltpu.make_async_copy(given[i], tables[i], table_sem.at[i]) for i in range(9)
    ]
    my_row = lax.axis_index("row")
    my_col = lax.axis_index("col")
    cols = lax.axis_size("col")
    me = my_row * cols + my_col

    def place(device):
        return (lax.div(device, cols), lax.rem(device, cols))

    def other(i):
        return lax.rem(me + i, DEVICES)

    barrier = pltpu.get_barrier_semaphore()

    def greet(i):
        pl.semaphore_signal(barrier, inc=1, device_id=place(other(i)), device_id_type=MESH)

    def greet_step(i, carry):
        for u in range(8):
            greet(i * 8 + u)
        return carry

    def load(group, slot):
        return pltpu.make_async_copy(
            fringes.at[at(group * GROUP, GROUP), :], block.at[slot], load_sem.at[slot]
        )

    def send(source, target, device, index):
        pltpu.make_async_remote_copy(
            src_ref=source, dst_ref=target, send_sem=send_sem.at[index],
            recv_sem=recv_sem.at[index], device_id=place(device), device_id_type=MESH,
        ).start()

    def keep(source, target, index):
        pltpu.make_async_copy(source, target, own_sem.at[index]).start()

    def wait_recv(buffer, index):
        others = buffer.at[pl.ds(0, DEVICES - 1)]
        pltpu.make_async_copy(others, others, recv_sem.at[index]).wait()
        pltpu.make_async_copy(buffer.at[0], buffer.at[0], own_sem.at[index]).wait()

    def wait_send(buffer, index):
        others = buffer.at[pl.ds(0, DEVICES - 1)]
        pltpu.make_async_copy(others, others, send_sem.at[index]).wait()

    load(0, 0).start()
    for copy in table_copies[:3]:
        copy.start()
    for i in range(1, 8):
        greet(i)
    lax.fori_loop(1, DEVICES // 8, greet_step, 0)

    table_copies[0].wait()
    table_copies[1].wait()

    def fill(i, carry):
        for u in range(8):
            twists[i * 8 + u] = jnp.broadcast_to(row_twist[pl.ds(i * 8 + u, 1), :], (8, 128))
        return carry

    lax.fori_loop(0, 64, fill, 0)

    def first_only(group):
        slot = lax.rem(group, 2)
        load(group + 1, 1 - slot).start()
        load(group, slot).wait()

        def piece(pair, carry):
            for rows16 in range(2):
                row_first(block.at[slot], pair, rows16, row_a, twists, mid.at[slot])
            return carry

        lax.fori_loop(0, 4, piece, 0)

    def both_steps(group, last):
        slot = lax.rem(group, 2)
        if not last:
            load(group + 1, 1 - slot).start()
        load(group, slot).wait()

        def piece(i, carry):
            row_second(
                mid.at[1 - slot], lax.div(i, 2), lax.rem(i, 2), row_b, lobe, lax.rem(group - 1, 4)
            )
            for rows16 in range(2):
                row_first(block.at[slot], i, rows16, row_a, twists, mid.at[slot])
            return carry

        lax.fori_loop(0, 4, piece, 0)

    def second_only(group):
        slot = lax.rem(group, 2)

        def piece(i, carry):
            row_second(mid.at[slot], lax.div(i, 2), lax.rem(i, 2), row_b, lobe, lax.rem(group, 4))
            return carry

        lax.fori_loop(0, 4, piece, 0)

    def send_block(buffer, target, k, low, index):
        for j in range(low, 4):
            device = k * 4 + lax.rem(me + j, 4)
            send(buffer.at[device], target.at[me], device, index)

    def quarter_step(c, carry):
        first_only(2 * c)

        @pl.when(c == 0)
        def _():
            table_copies[2].wait()

        both_steps(2 * c + 1, False)
        second_only(2 * c + 1)

        @pl.when(c == 0)
        def _():
            pl.semaphore_wait(barrier, DEVICES - 1)

        def pack(i):
            k = lax.rem(lax.div(me, 4) + i, 32)
            rows = at(c * 64, 64)
            upper = lobe[k, c, rows, :]
            lower = lobe[k, 1 - c, rows, :]
            flipped = jnp.concatenate([upper, lower], axis=0).T
            for j in range(4):
                send_a[c, k * 4 + j] = flipped[j * 32 : (j + 1) * 32]
            return k

        k = pack(0)
        keep(send_a.at[c, me], recv_a.at[c, me], c)
        send_block(send_a.at[c], recv_a.at[c], k, 1, c)

        def pack_step(i, inner):
            send_block(send_a.at[c], recv_a.at[c], pack(i), 0, c)
            return inner

        lax.fori_loop(1, 32, pack_step, 0)
        return carry

    lax.fori_loop(0, 2, quarter_step, 0)
    for copy in table_copies[3:]:
        copy.start()

    zone_rows[...] = jnp.zeros((8, 128), f32)
    zone_rows[0:4, 0:32] = zones[...]
    spread_rows = zone_rows[...]
    zone_row[...] = spread_rows[0:1] + sum(
        pltpu.roll(spread_rows, 32 * r, 1)[r : r + 1] for r in range(1, 4)
    )
    keep(zone_row, zones_out.at[me], 4)

    def send_zones(i, carry):
        send(zone_row, zones_out.at[me], other(i), 4)
        return carry

    first_only(4)

    def half_step(g, carry):
        both_steps(g, False)
        return carry

    lax.fori_loop(5, 7, half_step, 0)
    both_steps(7, True)
    second_only(7)

    def pack_half(i):
        k = lax.rem(lax.div(me, 4) + i, 32)
        for chunk in range(2):
            flipped = lobe[k, chunk].T
            for j in range(4):
                send_a[2 + chunk, k * 4 + j] = flipped[j * 32 : (j + 1) * 32]
        return k

    k = pack_half(0)
    keep(send_a.at[2, me], recv_a.at[2, me], 2)
    send_block(send_a.at[2], recv_a.at[2], k, 1, 2)

    def pack_half_step(i, carry):
        send_block(send_a.at[2], recv_a.at[2], pack_half(i), 0, 2)
        return carry

    lax.fori_loop(1, 32, pack_half_step, 0)
    keep(send_a.at[3, me], recv_a.at[3, me], 3)

    def send_last(i):
        send(send_a.at[3, other(i)], recv_a.at[3, me], other(i), 3)

    for i in range(1, 4):
        send_last(i)

    def last_step(i, carry):
        for u in range(4):
            send_last(i * 4 + u)
        return carry

    lax.fori_loop(1, DEVICES // 4, last_step, 0)
    lax.fori_loop(1, DEVICES, send_zones, 0)

    lanes = lax.broadcasted_iota(jnp.int32, (1, 256), 1)

    def edge_step(t, carry):
        mine = (lanes >= 4 * t) & (lanes < 4 * t + 4)
        return tuple(jnp.where(mine, bounds[side, t], carry[side]) for side in range(2))

    both = lax.fori_loop(0, 64, edge_step, (jnp.zeros((1, 256), jnp.int32),) * 2)
    edges[0] = both[0]
    edges[1] = both[1]

    first_column = lax.div(me, 4) + 32 * 32 * lax.rem(me, 4)
    low_lanes = lax.broadcasted_iota(jnp.int32, (32, 128), 1) < 64
    for copy in table_copies[3:]:
        copy.wait()
    wait_recv(recv_a.at[0], 0)
    wait_recv(recv_a.at[1], 1)
    for chunk in range(2):
        wait_recv(recv_a.at[2 + chunk], 2 + chunk)

        def spread(i, carry, chunk=chunk):
            for u in range(8):
                a = i * 8 + u
                early = recv_a[0, a].astype(f32)
                late = recv_a[1, a].astype(f32)
                if chunk == 0:
                    mine = jnp.where(low_lanes, early, late)
                else:
                    mine = pltpu.roll(jnp.where(low_lanes, late, early), 64, 1)
                gather[0, at(a * 32, 32), :] = mine
                gather[1, at(a * 32, 32), :] = recv_a[2 + chunk, a].astype(f32)
            return carry

        lax.fori_loop(0, DEVICES // 8, spread, 0)

        def column_step(index, carry, chunk=chunk):
            column_set(
                index, chunk, first_column, gather, (col_a, col_b, col_m, col_p),
                (col_twist, half_twist), edges, field,
            )
            return carry

        lax.fori_loop(0, 16 // COLUMNS, column_step, 0)

        def pack_field(i, chunk=chunk):
            device = other(i)
            for part in range(2):
                send_c[chunk, device, part * 16 : part * 16 + 16, :] = field[
                    pl.ds(part * 128 + device, 16, stride=256), :
                ].astype(bf16)
            return device

        def send_field(i, chunk=chunk):
            device = pack_field(i)
            send(send_c.at[chunk, device], out.at[chunk, me], device, 5 + chunk)

        pack_field(0)
        keep(send_c.at[chunk, me], out.at[chunk, me], 5 + chunk)
        for i in range(1, 4):
            send_field(i)

        def field_step(i, carry, chunk=chunk):
            for u in range(4):
                send_field(i * 4 + u)
            return carry

        lax.fori_loop(1, DEVICES // 4, field_step, 0)

    for index in range(4):
        wait_send(send_a.at[index], index)
    wait_send(zones_out, 4)
    wait_recv(zones_out, 4)
    for chunk in range(2):
        wait_send(send_c.at[chunk], 5 + chunk)
        wait_recv(out.at[chunk], 5 + chunk)


def exchange(lobe_bounds, fringes, zones, tables):
    names = ("row_a", "row_twist", "row_b", "col_a", "col_b", "col_m", "col_p", "col_twist", "half_twist")
    constants = [tables[name] for name in names]
    return pl.pallas_call(
        spectrum_kernel,
        out_shape=(
            jax.ShapeDtypeStruct((2, DEVICES, 32, KEPT), bf16),
            jax.ShapeDtypeStruct((DEVICES, 1, 128), f32),
        ),
        in_specs=[
            pl.BlockSpec(memory_space=pltpu.SMEM),
            pl.BlockSpec(memory_space=pltpu.HBM),
            pl.BlockSpec(memory_space=pltpu.VMEM),
        ]
        + [pl.BlockSpec(memory_space=pltpu.HBM)] * len(names),
        out_specs=(pl.BlockSpec(memory_space=pltpu.HBM),) * 2,
        scratch_shapes=[pltpu.VMEM(value.shape, value.dtype) for value in constants]
        + [
            pltpu.VMEM((2, GROUP, W), bf16),
            pltpu.VMEM((2, 2, 16, 16 * GROUP, 128), bf16),
            pltpu.VMEM((32, 2, HALF, 128), bf16),
            pltpu.VMEM((4, DEVICES, 32, 128), bf16),
            pltpu.VMEM((4, DEVICES, 32, 128), bf16),
            pltpu.VMEM((2, DEVICES * 32, 128), f32),
            pltpu.VMEM((16 * 256, 128), f32),
            pltpu.VMEM((2, DEVICES, 32, KEPT), bf16),
            pltpu.VMEM((2, 1, 256), jnp.int32),
            pltpu.VMEM((8, 128), f32),
            pltpu.VMEM((1, 128), f32),
            pltpu.VMEM((512, 8, 128), f32),
            pltpu.SemaphoreType.DMA((2,)),
            pltpu.SemaphoreType.DMA((7,)),
            pltpu.SemaphoreType.DMA((7,)),
            pltpu.SemaphoreType.DMA((7,)),
            pltpu.SemaphoreType.DMA((9,)),
        ],
        compiler_params=pltpu.CompilerParams(
            collective_id=0, has_side_effects=True, vmem_limit_bytes=60 << 20
        ),
        name="spectrum",
    )(lobe_bounds, fringes, zones, *constants)


def pixel_first(left, tile, half, pix_j, pix_twist, terms):
    mixed = dot(left, jnp.concatenate([pix_j[tile * 2], pix_j[tile * 2 + 1]], axis=1))
    for k0 in range(8):
        real = []
        imag = []
        for k1 in range(4):
            k = k1 * 8 + k0
            re = mixed[k * 16 : (k + 1) * 16, :128]
            im = mixed[k * 16 : (k + 1) * 16, 128:]
            if k:
                cosine = pix_twist[k, 0, tile]
                sine = pix_twist[k, 1, tile]
                cosine = jnp.concatenate([cosine, cosine], axis=0)
                sine = jnp.concatenate([sine, sine], axis=0)
                re, im = re * cosine - im * sine, im * cosine + re * sine
            real.append(re)
            imag.append(im)
        even_re, even_im = real[0] + real[2], imag[0] + imag[2]
        odd_re, odd_im = real[1] + real[3], imag[1] + imag[3]
        gap_re, gap_im = real[0] - real[2], imag[0] - imag[2]
        side_re, side_im = real[1] - real[3], imag[1] - imag[3]
        results = (
            (even_re + odd_re, even_im + odd_im),
            (gap_re - side_im, gap_im + side_re),
            (even_re - odd_re, even_im - odd_im),
            (gap_re + side_im, gap_im - side_re),
        )
        for p0 in range(4):
            for part in range(2):
                terms[p0, half, pl.ds(k0 * 32 + part * 16, 16), :] = results[p0][part].astype(bf16)


def pixel_second(group, q, pix_k, terms, zone_index, zone_table, pixels):
    for p0 in range(4):
        left = joined(pix_k.at[p0])
        mixed = [dot(left, joined(terms.at[u, p0])) for u in range(2)]
        for p1 in range(8):
            p = p0 + 4 * p1
            zone = zone_index[group, 2 * p + q // 2]
            source = lax.shift_right_logical(zone, 5)
            place = lax.bitwise_and(zone, 31)
            e0, e1, e2, e3 = (zone_table[source, place + 32 * r] for r in range(4))
            for u in range(2):
                real = mixed[u][p1 * 32 : p1 * 32 + 16]
                imag = mixed[u][p1 * 32 + 16 : p1 * 32 + 32]
                sine = imag * jnp.minimum(lax.rsqrt(real * real + imag * imag), 1.0 / damping_floor)
                heights = e0 + sine * (e1 + sine * (e2 + sine * e3))
                for h in range(2):
                    pixels[h * 8 : h * 8 + 8, pl.ds(1024 * p + (q + u) * 256, 256)] = heights[
                        h * 8 : h * 8 + 8
                    ].astype(bf16)


def height_kernel(
    zone_index, zone_table, received_in, pix_j_in, pix_twist_in, pix_k_in, out,
    received, pix_j, pix_twist, pix_k, rows, terms, pixels, store_sem, load_sem,
):
    loads = [
        pltpu.make_async_copy(source, target, load_sem.at[i])
        for i, (source, target) in enumerate(
            ((received_in, received), (pix_j_in, pix_j), (pix_twist_in, pix_twist), (pix_k_in, pix_k))
        )
    ]
    for copy in loads:
        copy.start()
    loads[0].wait()

    def flip(i, carry):
        for u in range(2):
            k = i * 2 + u
            for half in range(2):
                stacked = jnp.concatenate(
                    [
                        received[chunk, k * 4 + half * 2 + j]
                        for j in range(2)
                        for chunk in range(2)
                    ],
                    axis=0,
                )
                rows[k, half] = stacked.T
        return carry

    lax.fori_loop(0, 16, flip, 0)
    for copy in loads[1:]:
        copy.wait()
    groups = KEPT // ZB_R

    def store(group):
        slot = lax.rem(group, 2)
        return pltpu.make_async_copy(
            pixels.at[slot], out.at[at(group * ZB_R, ZB_R), :], store_sem.at[slot]
        )

    def front(group):
        left = jnp.concatenate(
            [rows[:, half, at(group * 16, 16), :].reshape(512, 128) for half in range(2)], axis=1
        )
        for q in range(4):
            for half in range(2):
                pixel_first(
                    left, q * 2 + half, half, pix_j, pix_twist, terms.at[lax.rem(group, 2), q]
                )

    def back(group):
        slot = lax.rem(group, 2)

        @pl.when(group >= 2)
        def _():
            store(group - 2).wait()

        for q in range(0, 4, 2):
            pixel_second(
                group, q, pix_k, terms.at[slot, pl.ds(q, 2)], zone_index, zone_table, pixels.at[slot]
            )

    front(0)

    def step(group, carry):
        back(group - 1)
        front(group)
        store(group - 1).start()
        return carry

    lax.fori_loop(1, groups, step, 0)
    back(groups - 1)
    store(groups - 1).start()
    store(groups - 2).wait()
    store(groups - 1).wait()


def height_map(zone_index, zone_table, received, tables):
    constants = [tables[name] for name in ("pix_j", "pix_twist", "pix_k")]
    return pl.pallas_call(
        height_kernel,
        out_shape=jax.ShapeDtypeStruct((KEPT, W), bf16),
        in_specs=[pl.BlockSpec(memory_space=pltpu.SMEM)] * 2
        + [pl.BlockSpec(memory_space=pltpu.HBM)] * 4,
        out_specs=pl.BlockSpec(memory_space=pltpu.HBM),
        scratch_shapes=[pltpu.VMEM(received.shape, received.dtype)]
        + [pltpu.VMEM(value.shape, value.dtype) for value in constants]
        + [
            pltpu.VMEM((32, 2, KEPT, 128), bf16),
            pltpu.VMEM((2, 4, 4, 2, 256, 128), bf16),
            pltpu.VMEM((2, ZB_R, W), bf16),
            pltpu.SemaphoreType.DMA((2,)),
            pltpu.SemaphoreType.DMA((4,)),
        ],
        compiler_params=pltpu.CompilerParams(vmem_limit_bytes=60 << 20),
        name="heights",
    )(zone_index, zone_table, received, *constants)


def body(tables, fringes, lobe_bounds, zone_index, zone_table):
    received, zones = exchange(lobe_bounds.T, fringes, zone_table, tables)
    return height_map(zone_index, zones.reshape(DEVICES, 128), received, tables)


def solution(mesh):
    placed = (P(("row", "col"), None), P(), P(("row", "col"), None), P(None, ("row", "col")))
    return jax.shard_map(
        functools.partial(body, make_tables()),
        mesh=mesh,
        in_specs=placed,
        out_specs=P(("row", "col"), None),
        check_vma=False,
    )
```
